256 devices in a mesh: grp: 8 (over z), seq: 32 (over y, x, core).
Axes of the slice: x: 4, y: 4, z: 8, core: 2. Of those that a mesh axis runs over, the one named last changes fastest.
Arguments:
- queries: bfloat16 [32768, 1232], P(('grp', 'seq')), may hold values from -6 to 6
- key_vectors: bfloat16 [32768, 1232], P(('grp', 'seq')), may hold values from -6 to 6
- value_vectors: bfloat16 [32768, 1232], P(('grp', 'seq')), may hold values from -1 to 3
- output_grad: bfloat16 [32768, 1232], P(('grp', 'seq')), may hold values from -12288 to 12288
- state_in: float32 [11, 112, 112], replicated, may hold values from 38.4 to 64
- norm_in: float32 [11, 112], replicated, may hold values from 38.4 to 64
- grad_state: float32 [11, 112, 112], replicated, may hold values from -1 to 1
- grad_norm: float32 [11, 112], replicated, may hold values from -12 to 12
Outputs:
- query_grad: bfloat16 [32768, 1232], P(('grp', 'seq'))
- key_grad: bfloat16 [32768, 1232], P(('grp', 'seq'))
- value_grad: bfloat16 [32768, 1232], P(('grp', 'seq'))
The draws below stay inside these ranges and needn't reach their ends.
All inputs are finite; a program needn't handle non-finite values.
Results may differ from the reference program's by a relative error of at most 0.006.
Values sent between devices are 32-bit elements; how exact they have to be, the bound alone decides.
A program may use at most 128 MiB of HBM per device.

```python
import jax
import jax.numpy as jnp
from jax import lax

HEADS = 11
HEAD = 112
TOK_DEV = 128
TOKENS = 32768


def shard_levels(stream_key, extent, split, smallest, top_value):
    factor_of, own = 1.0, jax.random.fold_in(stream_key, 6)
    for dim, parts in split:
        heights = jnp.exp(jax.random.uniform(jax.random.fold_in(own, dim), (parts,), jnp.float32, smallest / len(split), top_value / len(split)))
        factor_of = factor_of * jnp.repeat(heights, extent[dim] // parts).reshape([-1 if axis == dim else 1 for axis in range(len(extent))])
    return factor_of


def noise(stream_key, dims, scale, bound, pieces=(), held_as=jnp.bfloat16):
    drawn = jax.random.normal(stream_key, dims, jnp.float32) * scale
    if len(pieces) > 0:
        drawn = shard_levels(stream_key, dims, pieces, -0.22, 0.18) * drawn
    return jnp.clip(drawn, min=-bound, max=bound).astype(held_as)


def setup_inputs(seed: int = 0) -> dict:
    streams_of = jax.random.split(jax.random.key(seed), 9)
    queries = noise(streams_of[0], (TOKENS, HEADS * HEAD), 1.0, 6.0, ((0, 256),))
    key_vectors = noise(streams_of[1], (TOKENS, HEADS * HEAD), 1.0, 6.0, ((0, 256),))
    value_vectors = jnp.clip(-1.0 + 4.0 * jax.random.uniform(streams_of[2], (TOKENS, HEADS * HEAD), jnp.float32) ** shard_levels(streams_of[2], (TOKENS, HEADS * HEAD), ((0, 256),), -0.2, 0.2), -1.0, 3.0).astype(jnp.bfloat16)
    output_grad = noise(streams_of[3], (TOKENS, HEADS * HEAD), ((TOKENS * HEAD) ** 0.5), 12288.0, ((0, 256),))
    state_in = jnp.clip(jax.random.uniform(streams_of[4], (HEADS, HEAD, HEAD), jnp.float32, 38.4, 64.0), 38.4, 64.0)
    norm_in = jnp.clip(jax.random.uniform(streams_of[5], (HEADS, HEAD), jnp.float32, 38.4, 64.0), 38.4, 64.0)
    grad_state = noise(streams_of[6], (HEADS, HEAD, HEAD), (2.0 / HEAD ** 0.5), 1.0, (), jnp.float32)
    grad_norm = noise(streams_of[7], (HEADS, HEAD), 2.0, 12.0, (), jnp.float32)
    return dict(queries=queries, key_vectors=key_vectors, value_vectors=value_vectors, output_grad=output_grad, state_in=state_in, norm_in=norm_in, grad_state=grad_state, grad_norm=grad_norm)


def shifted_sum(blocks_data):
    running = jnp.cumsum(blocks_data, axis=0)
    return jnp.concatenate([jnp.zeros_like(blocks_data[:1]), running[:-1]], axis=0)


def later_sum(blocks_data):
    return jnp.flip(shifted_sum(jnp.flip(blocks_data, axis=0)), axis=0)


def head_grads(inputs):
    query_head, key_head, value_head, grad_head, state_head, norm_head, carry_head, carry_norm = inputs
    highest = lax.Precision.HIGHEST
    width = query_head.shape[1]
    blocks = query_head.shape[0] // TOK_DEV
    query_feat = jnp.maximum(query_head, 0).astype(jnp.float32).reshape(blocks, TOK_DEV, width)
    key_feat = jnp.maximum(key_head, 0).astype(jnp.float32).reshape(blocks, TOK_DEV, width)
    value_wide = value_head.astype(jnp.float32).reshape(blocks, TOK_DEV, width)
    grad_wide = grad_head.astype(jnp.float32).reshape(blocks, TOK_DEV, width)
    block_state = jnp.einsum('btd,bte->bde', key_feat, value_wide, precision=highest)
    block_norm = jnp.sum(key_feat, axis=1)
    prefix_state = state_head[None] + shifted_sum(block_state)
    prefix_norm = norm_head[None] + shifted_sum(block_norm)
    positions = lax.iota(jnp.int32, TOK_DEV)
    causal = (positions[:, None] >= positions[None, :])[None]
    masked = jnp.where(causal, jnp.einsum('btd,bsd->bts', query_feat, key_feat, precision=highest), 0.0)
    denominator = 1.0 + jnp.einsum('btd,bd->bt', query_feat, prefix_norm, precision=highest) + jnp.sum(masked, axis=2)
    scores_low = lax.optimization_barrier(masked.astype(jnp.bfloat16)).astype(jnp.float32)
    numerator = jnp.einsum('btd,bde->bte', query_feat, prefix_state, precision=highest) + jnp.einsum('bts,bse->bte', scores_low, value_wide, precision=highest)
    output = numerator / denominator[:, :, None]
    num_grad = grad_wide / denominator[:, :, None]
    den_grad = -jnp.sum(grad_wide * output, axis=2) / denominator
    num_grad_low = lax.optimization_barrier(num_grad.astype(jnp.bfloat16)).astype(jnp.float32)
    carry_state = jnp.einsum('btd,bte->bde', query_feat, num_grad_low, precision=highest)
    carry_sum = jnp.einsum('btd,bt->bd', query_feat, den_grad, precision=highest)
    suffix_state = carry_head[None] + later_sum(carry_state)
    suffix_norm = carry_norm[None] + later_sum(carry_sum)
    mixed = jnp.where(causal, jnp.einsum('bte,bse->bts', num_grad_low, value_wide, precision=highest) + den_grad[:, :, None], 0.0)
    mixed_low = lax.optimization_barrier(mixed.astype(jnp.bfloat16)).astype(jnp.float32)
    query_part = jnp.einsum('bte,bde->btd', num_grad, prefix_state, precision=highest) + den_grad[:, :, None] * prefix_norm[:, None, :] + jnp.einsum('bts,bsd->btd', mixed_low, key_feat, precision=highest)
    key_part = jnp.einsum('bse,bde->bsd', value_wide, suffix_state, precision=highest) + suffix_norm[:, None, :] + jnp.einsum('bts,btd->bsd', mixed_low, query_feat, precision=highest)
    value_part = jnp.einsum('bsd,bde->bse', key_feat, suffix_state, precision=highest) + jnp.einsum('bts,bte->bse', scores_low, num_grad_low, precision=highest)
    total = blocks * TOK_DEV
    query_grad = jnp.where(query_head > 0, query_part.reshape(total, width), 0.0).astype(jnp.bfloat16)
    key_grad = jnp.where(key_head > 0, key_part.reshape(total, width), 0.0).astype(jnp.bfloat16)
    value_grad = value_part.reshape(total, width).astype(jnp.bfloat16)
    return query_grad, key_grad, value_grad


def split_heads(array):
    return array.reshape(array.shape[0], HEADS, HEAD).transpose(1, 0, 2)


def join_heads(array):
    return array.transpose(1, 0, 2).reshape(array.shape[1], HEADS * HEAD)


def reference(queries, key_vectors, value_vectors, output_grad, state_in, norm_in, grad_state, grad_norm):
    results = lax.map(head_grads, (split_heads(queries), split_heads(key_vectors), split_heads(value_vectors), split_heads(output_grad), state_in, norm_in, grad_state, grad_norm))
    return (join_heads(results[0]), join_heads(results[1]), join_heads(results[2]))
```

```python
import functools
import math

import jax
import jax.numpy as jnp
from jax import lax
from jax.experimental import pallas as pl
from jax.experimental.pallas import tpu as pltpu
from jax.sharding import PartitionSpec as P

MESH = pl.DeviceIdType.MESH
F32 = jnp.float32
BF16 = jnp.bfloat16
NN = (((1,), (0,)), ((), ()))
NT = (((1,), (1,)), ((), ()))
TN = (((0,), (0,)), ((), ()))
LANES = 128


def mm(x, y, dims):
    return lax.dot_general(x, y, dims, preferred_element_type=F32)


def split(x):
    high = x.astype(BF16)
    return high, (x - high.astype(F32)).astype(BF16)


class Place:
    def __init__(self, groups, chips):
        self.groups, self.chips = groups, chips
        self.side = math.isqrt(chips)
        self.z = lax.axis_index("grp")
        seq = lax.axis_index("seq")
        self.p, self.c = seq // 2, seq % 2
        self.y, self.x = self.p // self.side, self.p % self.side
        side = self.side
        offsets = [(dy, dx) for dy in range(side) for dx in range(side) if dy or dx]
        self.plane = sorted(offsets, key=lambda o: min(o[0], side - o[0]) + min(o[1], side - o[1]))
        self.column = sorted(range(1, groups), key=lambda d: min(d, groups - d))

    def chip(self, offset, sign):
        side = self.side
        y = (self.y + sign * offset[0] + side) % side
        x = (self.x + sign * offset[1] + side) % side
        return y * side + x

    def plane_to(self, k):
        return self.chip(self.plane[k], 1)

    def plane_from(self, k):
        return self.chip(self.plane[k], -1)

    def z_to(self, k):
        return (self.z + self.column[k]) % self.groups

    def z_from(self, k):
        return (self.z + self.groups - self.column[k]) % self.groups

    def chip_id(self, p):
        return (self.z, p * 2 + self.c)

    def z_id(self, z):
        return (z, self.p * 2 + self.c)

    def core_id(self):
        return (self.z, self.p * 2 + 1 - self.c)


def remote(src, dst, send, recv, device):
    return pltpu.make_async_remote_copy(
        src_ref=src, dst_ref=dst, send_sem=send, recv_sem=recv, device_id=device, device_id_type=MESH
    )


def flag(condition):
    return condition.astype(jnp.int32).astype(F32)


class SmallScan:
    def __init__(self, at, later, refs):
        self.at, self.later = at, later
        self.own, self.other, self.chip, self.plane, self.column, self.total = refs[:6]
        self.core_s, self.plane_s, self.column_s = refs[6:]
        self.sent = []

    def start(self, copy):
        copy.start()
        self.sent.append(copy)

    def core_copy(self):
        sems = self.core_s
        return remote(self.own, self.other, sems.at[0, 0], sems.at[1, 0], self.at.core_id())

    def core_send(self):
        self.start(self.core_copy())

    def plane_copy(self, k, slot, device):
        sems = self.plane_s
        return remote(self.chip, self.plane.at[slot], sems.at[0, k], sems.at[1, k], device)

    def plane_send(self):
        at = self.at
        self.core_copy().wait_recv()
        both = self.own[...] + self.other[...]
        self.chip[...] = both
        for k in reversed(range(len(at.plane))):
            self.start(self.plane_copy(k, at.p, at.chip_id(at.plane_to(k))))
        self.plane[at.p] = both

    def column_copy(self, k, slot, device):
        sems = self.column_s
        return remote(
            self.column.at[self.at.z], self.column.at[slot], sems.at[0, k], sems.at[1, k], device
        )

    def column_send(self):
        at = self.at
        for k in range(len(at.plane)):
            source = at.plane_from(k)
            self.plane_copy(k, source, at.chip_id(source)).wait_recv()
        everything = self.plane[0]
        for p in range(1, at.chips):
            everything = everything + self.plane[p]
        self.column[at.z] = everything
        for k in reversed(range(len(at.column))):
            self.start(self.column_copy(k, at.z, at.z_id(at.z_to(k))))
        reached = (lambda i, me: i > me) if self.later else (lambda i, me: i < me)
        near = flag(at.c == (0 if self.later else 1)) * self.other[...]
        for p in range(at.chips):
            near = near + flag(reached(p, at.p)) * self.plane[p]
        self.total[...] = self.total[...] + near

    def finish(self):
        at = self.at
        for k in range(len(at.column)):
            source = at.z_from(k)
            self.column_copy(k, source, at.z_id(source)).wait_recv()
        reached = (lambda i, me: i > me) if self.later else (lambda i, me: i < me)
        far = flag(reached(0, at.z)) * self.column[0]
        for z in range(1, at.groups):
            far = far + flag(reached(z, at.z)) * self.column[z]
        self.total[...] = self.total[...] + far

    def drain(self):
        for copy in self.sent:
            copy.wait_send()


class LargeScan:
    def __init__(self, at, later, share, refs):
        self.at, self.later, self.share = at, later, share
        self.own, self.other, self.chip, self.plane, self.column, self.back, self.result = refs[:7]
        self.core_s, self.plane_s, self.column_s, self.back_s, self.pass_s = refs[7:]
        self.half = share * at.chips
        self.sent = []

    def start(self, copy):
        copy.start()
        self.sent.append(copy)

    def piece(self, p):
        return pl.ds((self.at.c * self.at.chips + p) * self.share, self.share)

    def core_copy(self, k, core):
        part = pl.ds(core * self.half, self.half)
        sems = self.core_s
        return remote(
            self.own.at[part], self.other.at[part], sems.at[0, k], sems.at[1, k], self.at.core_id()
        )

    def core_send(self):
        self.start(self.core_copy(0, 1 - self.at.c))
        self.start(self.core_copy(1, self.at.c))

    def plane_copy(self, k, src, slot, device):
        sems = self.plane_s
        return remote(self.chip.at[src], self.plane.at[slot], sems.at[0, k], sems.at[1, k], device)

    def plane_send(self):
        at = self.at
        self.core_copy(0, at.c).wait_recv()
        for k in reversed(range(len(at.plane))):
            target = at.plane_to(k)
            part = self.piece(target)
            self.chip[target] = self.own[part] + self.other[part]
            self.start(self.plane_copy(k, target, at.p, at.chip_id(target)))
        part = self.piece(at.p)
        self.plane[at.p] = self.own[part] + self.other[part]

    def column_copy(self, k, slot, device):
        sems = self.column_s
        return remote(
            self.column.at[self.at.z], self.column.at[slot], sems.at[0, k], sems.at[1, k], device
        )

    def column_send(self):
        at = self.at
        for k in range(len(at.plane)):
            source = at.plane_from(k)
            self.plane_copy(k, source, source, at.chip_id(source)).wait_recv()
        order = list(range(at.chips))
        if self.later:
            order.reverse()
        running = jnp.zeros(self.column.shape[1:], F32)
        for p in order:
            self.back[p] = running
            running = running + self.plane[p]
        self.column[at.z] = running
        for k in reversed(range(len(at.column))):
            self.start(self.column_copy(k, at.z, at.z_id(at.z_to(k))))

    def back_copy(self, k, src, owner, device):
        sems = self.back_s
        return remote(
            self.back.at[src], self.result.at[self.piece(owner)], sems.at[0, k], sems.at[1, k], device
        )

    def pass_copy(self, k, core, owner):
        part = pl.ds((core * self.at.chips + owner) * self.share, self.share)
        sems = self.pass_s
        return remote(
            self.result.at[part], self.result.at[part], sems.at[0, k], sems.at[1, k], self.at.core_id()
        )

    def back_send(self):
        at = self.at
        for k in range(len(at.column)):
            source = at.z_from(k)
            self.column_copy(k, source, at.z_id(source)).wait_recv()
        reached = (lambda i, me: i > me) if self.later else (lambda i, me: i < me)
        far = flag(reached(0, at.z)) * self.column[0]
        for z in range(1, at.groups):
            far = far + flag(reached(z, at.z)) * self.column[z]
        for k in reversed(range(len(at.plane))):
            target = at.plane_to(k)
            self.back[target] = self.back[target] + far
            self.start(self.back_copy(k, target, at.p, at.chip_id(target)))
        self.result[self.piece(at.p)] = self.back[at.p] + far
        self.start(self.pass_copy(len(at.plane), at.c, at.p))

    def back_pass(self):
        at = self.at
        for k in range(len(at.plane)):
            source = at.plane_from(k)
            self.back_copy(k, source, source, at.chip_id(source)).wait_recv()
            self.start(self.pass_copy(k, at.c, source))

    def core_rest(self):
        self.core_copy(1, 1 - self.at.c).wait_recv()

    def finish(self):
        at = self.at
        for k in range(len(at.plane)):
            self.pass_copy(k, 1 - at.c, at.plane_from(k)).wait_recv()
        self.pass_copy(len(at.plane), 1 - at.c, at.p).wait_recv()

    def drain(self):
        for copy in self.sent:
            copy.wait_send()


def kernel(groups, chips, heads, width, share, *refs):
    hbm_in, hbm_out, refs = refs[:8], refs[8:11], refs[11:]
    q_v, k_v, v_v, g_v, st_v, nm_v, gs_v, gn_v = refs[:8]
    dq_v, dk_v, dv_v = refs[8:11]
    a_s, b_s, v_s, g_s, ub_s, ul_s, ua_s, pt_s, sh_s, sl_s, rh_s, rl_s = refs[11:23]
    den_s, num_s, c_s, kp_s, vp_s, init_s, init_r = refs[23:30]
    load_s, store_s = refs[30:32]
    small = refs[32:50]
    large = refs[50:]
    at = Place(groups, chips)
    n_scan = SmallScan(at, False, small[:9])
    m_scan = SmallScan(at, True, small[9:])
    b_scan = LargeScan(at, False, share, large[:12])
    c_scan = LargeScan(at, True, share, large[12:])
    tokens = k_v.shape[0]
    rows = width // 8

    barrier = pltpu.get_barrier_semaphore()
    for k in range(len(at.plane)):
        pl.semaphore_signal(
            barrier, inc=1, device_id=at.chip_id(at.plane_to(k)), device_id_type=MESH
        )
    for k in range(len(at.column)):
        pl.semaphore_signal(barrier, inc=1, device_id=at.z_id(at.z_to(k)), device_id_type=MESH)
    pl.semaphore_signal(barrier, inc=1, device_id=at.core_id(), device_id_type=MESH)

    loads = [
        pltpu.make_async_copy(src, dst, load_s.at[i])
        for i, (src, dst) in enumerate(zip(hbm_in, (q_v, k_v, v_v, g_v, st_v, nm_v, gs_v, gn_v)))
    ]
    for i in (1, 2, 0, 3, 5, 4, 7, 6):
        loads[i].start()

    lane = lax.broadcasted_iota(jnp.int32, (tokens, LANES), 1)
    row = lax.broadcasted_iota(jnp.int32, (tokens, LANES), 0)
    lower = row >= lane
    upper = row <= lane
    ones_pair = jnp.where((lane == width) | (lane == width + 1), 1.0, 0.0).astype(BF16)
    blank = jnp.zeros((tokens, LANES), BF16)
    for h in range(heads):
        a_s[h] = blank
        b_s[h] = blank
        v_s[h] = ones_pair
        g_s[h] = blank
        for ref in (sh_s, sl_s, rh_s, rl_s):
            ref[h, width:, :] = jnp.zeros((LANES - width, LANES), BF16)
    spare = b_scan.own.shape[0] - heads * rows
    for scan in (b_scan, c_scan):
        scan.own[heads * rows :] = jnp.zeros((spare, 8, LANES), F32)
    for scan in (n_scan, m_scan):
        scan.own[...] = jnp.zeros(scan.own.shape, F32)
        scan.total[...] = jnp.zeros(scan.own.shape, F32)

    def tiles(h):
        return slice(h * rows, (h + 1) * rows)

    def columns(h):
        return slice(h * width, (h + 1) * width)

    loads[1].wait()
    for h in range(heads):
        b_s[h, :, :width] = jnp.maximum(k_v[:, columns(h)], 0)
    some = jnp.ones((8, tokens), BF16)
    for h in range(heads):
        n_scan.own[h : h + 1, :] = mm(some, b_s[h], NN)[0:1]
    pl.semaphore_wait(barrier, len(at.plane) + len(at.column) + 1)
    n_scan.core_send()

    loads[2].wait()
    for h in range(heads):
        v_s[h, :, :width] = v_v[:, columns(h)]
    for h in range(heads):
        b_scan.own[tiles(h)] = mm(b_s[h], v_s[h], TN)[:width].reshape(rows, 8, LANES)
    b_scan.core_send()
    n_scan.plane_send()

    loads[0].wait()
    for h in range(heads):
        a_s[h, :, :width] = jnp.maximum(q_v[:, columns(h)], 0)
    b_scan.plane_send()

    loads[5].wait()
    n_scan.total[:heads, :width] = nm_v[...]
    loads[7].wait()
    m_scan.total[:heads, :width] = gn_v[...]

    loads[3].wait()
    for h in range(heads):
        g_s[h, :, :width] = g_v[:, columns(h)]
    for h in range(heads):
        scores = jnp.where(lower, mm(a_s[h], b_s[h], NT), 0.0)
        den_s[h] = jnp.broadcast_to(1.0 + jnp.sum(scores, axis=1, keepdims=True), (tokens, LANES))
        num_s[h] = mm(scores.astype(BF16), v_s[h], NN)
        pt_s[h] = jnp.where(upper, mm(b_s[h], a_s[h], NT), 0.0).astype(BF16)
    n_scan.column_send()

    loads[4].wait()
    loads[6].wait()
    for init, state in ((init_s, st_v), (init_r, gs_v)):
        init[...] = jnp.zeros(init.shape, F32)
        for h in range(heads):
            init[tiles(h), :, :width] = state[h].reshape(rows, 8, width)
    b_scan.core_rest()
    init_s[...] = init_s[...] + flag(at.c == 1) * b_scan.other[: heads * rows]

    b_scan.column_send()

    n_scan.finish()
    for h in range(heads):
        high, low = split(n_scan.total[h : h + 1, :])
        both = mm(a_s[h], jnp.broadcast_to(high, (LANES, LANES)), NT) + mm(
            a_s[h], jnp.broadcast_to(low, (LANES, LANES)), NT
        )
        inverse = 1.0 / (den_s[h] + both)
        den_s[h] = inverse
        ub_s[h], ul_s[h] = split(g_s[h].astype(F32) * inverse)
    for h in range(heads):
        c_scan.own[tiles(h)] = mm(a_s[h], ub_s[h], TN)[:width].reshape(rows, 8, LANES)
    c_scan.core_send()
    for h in range(heads):
        vp_s[h] = mm(pt_s[h], ub_s[h], NN)
    c_scan.plane_send()
    b_scan.back_send()
    c_scan.core_rest()
    init_r[...] = init_r[...] + flag(at.c == 0) * c_scan.other[: heads * rows]
    b_scan.back_pass()
    c_scan.column_send()
    b_scan.finish()

    for h in range(heads):
        state = (b_scan.result[tiles(h)] + init_s[tiles(h)]).reshape(width, LANES)
        sh_s[h, :width, :], sl_s[h, :width, :] = split(state)
    for h in range(heads):
        numerator = mm(a_s[h], sh_s[h], NN) + mm(a_s[h], sl_s[h], NN) + num_s[h]
        inverse = den_s[h]
        scaled = g_s[h].astype(F32) * inverse
        c = -jnp.sum(scaled * (numerator * inverse), axis=1, keepdims=True)
        c_s[h] = jnp.broadcast_to(c, (tokens, LANES))
        m_scan.own[h : h + 1, :] = jnp.sum(c * a_s[h].astype(F32), axis=0, keepdims=True)
    m_scan.core_send()
    m_scan.plane_send()

    for h in range(heads):
        high, low = split(c_s[h])
        ua_s[h] = jnp.where(lane == width, high, jnp.where(lane == width + 1, low, ub_s[h]))
    for h in range(heads):
        mixed = jnp.where(lower, mm(ua_s[h], v_s[h], NT), 0.0).astype(BF16)
        part = mm(ub_s[h], sh_s[h], NT) + mm(ub_s[h], sl_s[h], NT) + mm(ul_s[h], sh_s[h], NT)
        part = part + c_s[h] * n_scan.total[h : h + 1, :] + mm(mixed, b_s[h], NN)
        part = jnp.where(a_s[h] > 0, part, 0.0)
        dq_v[:, columns(h)] = part[:, :width].astype(BF16)
        turned = jnp.where(upper, mm(v_s[h], ua_s[h], NT), 0.0).astype(BF16)
        kp_s[h] = mm(turned, a_s[h], NN)
    stores = [
        pltpu.make_async_copy(src, dst, store_s.at[i])
        for i, (src, dst) in enumerate(zip((dq_v, dk_v, dv_v), hbm_out))
    ]
    stores[0].start()
    c_scan.back_send()
    m_scan.column_send()
    c_scan.back_pass()
    c_scan.finish()

    for h in range(heads):
        state = (c_scan.result[tiles(h)] + init_r[tiles(h)]).reshape(width, LANES)
        rh_s[h, :width, :], rl_s[h, :width, :] = split(state)
    for h in range(heads):
        part = vp_s[h] + mm(b_s[h], rh_s[h], NN) + mm(b_s[h], rl_s[h], NN)
        dv_v[:, columns(h)] = part[:, :width].astype(BF16)
    stores[2].start()
    for h in range(heads):
        kp_s[h] = kp_s[h] + mm(v_s[h], rh_s[h], NT) + mm(v_s[h], rl_s[h], NT)
    m_scan.finish()
    for h in range(heads):
        part = jnp.where(b_s[h] > 0, kp_s[h] + m_scan.total[h : h + 1, :], 0.0)
        dk_v[:, columns(h)] = part[:, :width].astype(BF16)
    stores[1].start()
    for scan in (n_scan, b_scan, m_scan, c_scan):
        scan.drain()
    for copy in stores:
        copy.wait()


def small_scratch(groups, chips):
    one = pltpu.VMEM((16, LANES), F32)
    sem = pltpu.SemaphoreType.DMA
    return [
        one,
        one,
        one,
        pltpu.VMEM((chips, 16, LANES), F32),
        pltpu.VMEM((groups, 16, LANES), F32),
        one,
        sem((2, 1)),
        sem((2, chips - 1)),
        sem((2, groups - 1)),
    ]


def large_scratch(groups, chips, share):
    whole = pltpu.VMEM((2 * chips * share, 8, LANES), F32)
    plane = pltpu.VMEM((chips, share, 8, LANES), F32)
    sem = pltpu.SemaphoreType.DMA
    return [
        whole,
        whole,
        plane,
        plane,
        pltpu.VMEM((groups, share, 8, LANES), F32),
        plane,
        whole,
        sem((2, 2)),
        sem((2, chips - 1)),
        sem((2, groups - 1)),
        sem((2, chips - 1)),
        sem((2, chips)),
    ]


def per_device(groups, chips, *args):
    tokens, columns = args[0].shape
    heads, width = args[4].shape[:2]
    share = -(-(heads * width // 8) // (2 * chips))
    token = pltpu.VMEM((tokens, columns), BF16)
    state = pltpu.VMEM((heads, width, width), F32)
    norm = pltpu.VMEM((heads, width), F32)
    low = pltpu.VMEM((heads, tokens, LANES), BF16)
    square = pltpu.VMEM((heads, LANES, LANES), BF16)
    wide = pltpu.VMEM((heads, tokens, LANES), F32)
    init = pltpu.VMEM((heads * width // 8, 8, LANES), F32)
    sem = pltpu.SemaphoreType.DMA
    scratch = [token] * 4 + [state, norm, state, norm] + [token] * 3
    scratch += [low] * 7 + [square] + [square] * 4
    scratch += [wide] * 5 + [init] * 2 + [sem((8,)), sem((3,))]
    scratch += small_scratch(groups, chips) * 2 + large_scratch(groups, chips, share) * 2
    return pl.pallas_call(
        functools.partial(kernel, groups, chips, heads, width, share),
        out_shape=[jax.ShapeDtypeStruct((tokens, columns), BF16)] * 3,
        in_specs=[pl.BlockSpec(memory_space=pl.ANY)] * 8,
        out_specs=[pl.BlockSpec(memory_space=pl.ANY)] * 3,
        scratch_shapes=scratch,
        compiler_params=pltpu.CompilerParams(
            collective_id=0, has_side_effects=True, vmem_limit_bytes=40 * 2**20
        ),
        name="scan_kernel",
    )(*args)


def solution(mesh):
    groups, chips = mesh.shape["grp"], mesh.shape["seq"] // 2
    tokens = P(("grp", "seq"), None)
    return jax.shard_map(
        functools.partial(per_device, groups, chips),
        mesh=mesh,
        in_specs=(tokens,) * 4 + (P(),) * 4,
        out_specs=(tokens,) * 3,
        check_vma=False,
    )
```

```python
import functools
import math

import jax
import jax.numpy as jnp
from jax import lax
from jax.experimental import pallas as pl
from jax.experimental.pallas import tpu as pltpu
from jax.sharding import PartitionSpec as P

MESH = pl.DeviceIdType.MESH
F32 = jnp.float32
BF16 = jnp.bfloat16
NN = (((1,), (0,)), ((), ()))
NT = (((1,), (1,)), ((), ()))
TN = (((0,), (0,)), ((), ()))
LANES = 128


def mm(x, y, dims):
    return lax.dot_general(x, y, dims, preferred_element_type=F32)


def split(x):
    high = x.astype(BF16)
    return high, (x - high.astype(F32)).astype(BF16)


class Place:
    def __init__(self, groups, chips):
        self.groups, self.chips = groups, chips
        self.side = math.isqrt(chips)
        self.z = lax.axis_index("grp")
        seq = lax.axis_index("seq")
        self.p, self.c = seq // 2, seq % 2
        self.y, self.x = self.p // self.side, self.p % self.side
        side = self.side
        offsets = [(dy, dx) for dy in range(side) for dx in range(side) if dy or dx]
        self.plane = sorted(offsets, key=lambda o: min(o[0], side - o[0]) + min(o[1], side - o[1]))
        self.column = sorted(range(1, groups), key=lambda d: min(d, groups - d))

    def chip(self, offset, sign):
        side = self.side
        y = (self.y + sign * offset[0] + side) % side
        x = (self.x + sign * offset[1] + side) % side
        return y * side + x

    def plane_to(self, k):
        return self.chip(self.plane[k], 1)

    def plane_from(self, k):
        return self.chip(self.plane[k], -1)

    def z_to(self, k):
        return (self.z + self.column[k]) % self.groups

    def z_from(self, k):
        return (self.z + self.groups - self.column[k]) % self.groups

    def chip_id(self, p):
        return (self.z, p * 2 + self.c)

    def z_id(self, z):
        return (z, self.p * 2 + self.c)

    def core_id(self):
        return (self.z, self.p * 2 + 1 - self.c)


def remote(src, dst, send, recv, device):
    return pltpu.make_async_remote_copy(
        src_ref=src, dst_ref=dst, send_sem=send, recv_sem=recv, device_id=device, device_id_type=MESH
    )


def flag(condition):
    return condition.astype(jnp.int32).astype(F32)


class SmallScan:
    def __init__(self, at, later, refs):
        self.at, self.later = at, later
        self.own, self.other, self.chip, self.plane, self.column, self.total, self.flat = refs[:7]
        self.core_s, self.plane_s, self.column_s = refs[7:]
        self.sent = []

    def start(self, copy):
        copy.start()
        self.sent.append(copy)

    def core_copy(self):
        sems = self.core_s
        return remote(self.own, self.other, sems.at[0, 0], sems.at[1, 0], self.at.core_id())

    def core_send(self):
        self.start(self.core_copy())

    def plane_copy(self, k, slot, device):
        sems = self.plane_s
        return remote(self.chip, self.plane.at[slot], sems.at[0, k], sems.at[1, k], device)

    def plane_send(self):
        at = self.at
        self.core_copy().wait_recv()
        both = self.own[...] + self.other[...]
        self.chip[...] = both
        for k in reversed(range(len(at.plane))):
            self.start(self.plane_copy(k, at.p, at.chip_id(at.plane_to(k))))
        self.plane[at.p] = both

    def column_copy(self, k, slot, device):
        sems = self.column_s
        return remote(
            self.column.at[self.at.z], self.column.at[slot], sems.at[0, k], sems.at[1, k], device
        )

    def column_send(self):
        at = self.at
        for k in range(len(at.plane)):
            source = at.plane_from(k)
            self.plane_copy(k, source, at.chip_id(source)).wait_recv()
        everything = self.plane[0]
        for p in range(1, at.chips):
            everything = everything + self.plane[p]
        self.column[at.z] = everything
        for k in reversed(range(len(at.column))):
            self.start(self.column_copy(k, at.z, at.z_id(at.z_to(k))))
        reached = (lambda i, me: i > me) if self.later else (lambda i, me: i < me)
        near = flag(at.c == (0 if self.later else 1)) * self.other[...]
        for p in range(at.chips):
            near = near + flag(reached(p, at.p)) * self.plane[p]
        self.total[...] = self.total[...] + near

    def finish(self):
        at = self.at
        for k in range(len(at.column)):
            source = at.z_from(k)
            self.column_copy(k, source, at.z_id(source)).wait_recv()
        reached = (lambda i, me: i > me) if self.later else (lambda i, me: i < me)
        far = flag(reached(0, at.z)) * self.column[0]
        for z in range(1, at.groups):
            far = far + flag(reached(z, at.z)) * self.column[z]
        self.total[...] = self.total[...] + far
        for h in range(self.total.shape[0]):
            self.flat[h : h + 1, :] = self.total[h]

    def drain(self):
        for copy in self.sent:
            copy.wait_send()


class LargeScan:
    def __init__(self, at, later, share, refs):
        self.at, self.later, self.share = at, later, share
        self.own, self.other, self.chip, self.plane, self.column, self.back, self.result = refs[:7]
        self.core_s, self.plane_s, self.column_s, self.back_s, self.pass_s = refs[7:]
        self.half = share * at.chips
        self.sent = []

    def start(self, copy):
        copy.start()
        self.sent.append(copy)

    def piece(self, p):
        return pl.ds((self.at.c * self.at.chips + p) * self.share, self.share)

    def core_copy(self, k, core):
        part = pl.ds(core * self.half, self.half)
        sems = self.core_s
        return remote(
            self.own.at[part], self.other.at[part], sems.at[0, k], sems.at[1, k], self.at.core_id()
        )

    def core_send(self):
        self.start(self.core_copy(0, 1 - self.at.c))
        self.start(self.core_copy(1, self.at.c))

    def plane_copy(self, k, src, slot, device):
        sems = self.plane_s
        return remote(self.chip.at[src], self.plane.at[slot], sems.at[0, k], sems.at[1, k], device)

    def plane_send(self):
        at = self.at
        self.core_copy(0, at.c).wait_recv()
        for k in reversed(range(len(at.plane))):
            target = at.plane_to(k)
            part = self.piece(target)
            self.chip[target] = self.own[part] + self.other[part]
            self.start(self.plane_copy(k, target, at.p, at.chip_id(target)))
        part = self.piece(at.p)
        self.plane[at.p] = self.own[part] + self.other[part]

    def column_copy(self, k, slot, device):
        sems = self.column_s
        return remote(
            self.column.at[self.at.z], self.column.at[slot], sems.at[0, k], sems.at[1, k], device
        )

    def column_send(self):
        at = self.at
        for k in range(len(at.plane)):
            source = at.plane_from(k)
            self.plane_copy(k, source, source, at.chip_id(source)).wait_recv()
        order = list(range(at.chips))
        if self.later:
            order.reverse()
        running = jnp.zeros(self.column.shape[1:], F32)
        for p in order:
            self.back[p] = running
            running = running + self.plane[p]
        self.column[at.z] = running
        for k in reversed(range(len(at.column))):
            self.start(self.column_copy(k, at.z, at.z_id(at.z_to(k))))

    def back_copy(self, k, src, owner, device):
        sems = self.back_s
        return remote(
            self.back.at[src], self.result.at[self.piece(owner)], sems.at[0, k], sems.at[1, k], device
        )

    def pass_copy(self, k, core, owner):
        part = pl.ds((core * self.at.chips + owner) * self.share, self.share)
        sems = self.pass_s
        return remote(
            self.result.at[part], self.result.at[part], sems.at[0, k], sems.at[1, k], self.at.core_id()
        )

    def back_send(self):
        at = self.at
        for k in range(len(at.column)):
            source = at.z_from(k)
            self.column_copy(k, source, at.z_id(source)).wait_recv()
        reached = (lambda i, me: i > me) if self.later else (lambda i, me: i < me)
        far = flag(reached(0, at.z)) * self.column[0]
        for z in range(1, at.groups):
            far = far + flag(reached(z, at.z)) * self.column[z]
        for k in reversed(range(len(at.plane))):
            target = at.plane_to(k)
            self.back[target] = self.back[target] + far
            self.start(self.back_copy(k, target, at.p, at.chip_id(target)))
        self.result[self.piece(at.p)] = self.back[at.p] + far
        self.start(self.pass_copy(len(at.plane), at.c, at.p))

    def back_pass(self):
        at = self.at
        for k in range(len(at.plane)):
            source = at.plane_from(k)
            self.back_copy(k, source, source, at.chip_id(source)).wait_recv()
            self.start(self.pass_copy(k, at.c, source))

    def core_rest(self):
        self.core_copy(1, 1 - self.at.c).wait_recv()

    def finish(self):
        at = self.at
        for k in range(len(at.plane)):
            self.pass_copy(k, 1 - at.c, at.plane_from(k)).wait_recv()
        self.pass_copy(len(at.plane), 1 - at.c, at.p).wait_recv()

    def drain(self):
        for copy in self.sent:
            copy.wait_send()


def kernel(groups, chips, heads, width, share, *refs):
    hbm_in, (dq_v, dk_v, dv_v), refs = refs[:8], refs[8:11], refs[11:]
    q_v, k_v, v_v, g_v, st_v, nm_v, gs_v, gn_v = refs[:8]
    a_s, b_s, ub_s, ul_s, sh_s, sl_s, pt_s = refs[8:15]
    num_s, kp_s, vp_s, den_s, c_s, init_s, init_r = refs[15:22]
    load_s = refs[22]
    small = refs[23:43]
    large = refs[43:]
    at = Place(groups, chips)
    n_scan = SmallScan(at, False, small[:10])
    m_scan = SmallScan(at, True, small[10:])
    b_scan = LargeScan(at, False, share, large[:12])
    c_scan = LargeScan(at, True, share, large[12:])
    tokens = k_v.shape[1]
    tall = width // 8

    loads = [
        pltpu.make_async_copy(src, dst, load_s.at[i])
        for i, (src, dst) in enumerate(zip(hbm_in, (q_v, k_v, v_v, g_v, st_v, nm_v, gs_v, gn_v)))
    ]
    loads[1].start()
    loads[2].start()
    barrier = pltpu.get_barrier_semaphore()
    partners = [at.core_id()]
    partners += [at.chip_id(at.plane_to(k)) for k in range(len(at.plane))]
    partners += [at.z_id(at.z_to(k)) for k in range(len(at.column))]
    for partner in partners:
        pl.semaphore_signal(barrier, inc=1, device_id=partner, device_id_type=MESH)
    for i in (0, 3, 5, 7, 4, 6):
        loads[i].start()

    upper = lax.broadcasted_iota(jnp.int32, (tokens, tokens), 0) <= lax.broadcasted_iota(
        jnp.int32, (tokens, tokens), 1
    )
    for scan in (b_scan, c_scan):
        scan.own[...] = jnp.zeros(scan.own.shape, F32)
    for scan in (n_scan, m_scan):
        scan.own[...] = jnp.zeros(scan.own.shape, F32)
        scan.total[...] = jnp.zeros(scan.total.shape, F32)
        scan.flat[...] = jnp.zeros(scan.flat.shape, F32)
    den_s[...] = jnp.ones(den_s.shape, F32)
    c_s[...] = jnp.zeros(c_s.shape, F32)

    def tiles(h):
        return slice(h * tall, (h + 1) * tall)

    def rows(h):
        return slice(h * width, (h + 1) * width)

    loads[1].wait()
    b_s[...] = jnp.maximum(k_v[...], 0)
    some = jnp.ones((16, tokens), BF16)
    for h in range(heads):
        n_scan.own[h, :, :width] = mm(some, b_s[rows(h)], NT)[0:1]
    pl.semaphore_wait(barrier, len(partners))
    n_scan.core_send()

    loads[2].wait()
    for h in range(heads):
        state = mm(v_v[rows(h)], b_s[rows(h)], NT)
        b_scan.own[tiles(h), :, :width] = state.reshape(tall, 8, width)
    b_scan.core_send()
    n_scan.plane_send()

    loads[0].wait()
    a_s[...] = jnp.maximum(q_v[...], 0)
    b_scan.plane_send()

    loads[5].wait()
    loads[7].wait()
    for h in range(heads):
        n_scan.total[h, :, :width] = nm_v[h : h + 1]
        m_scan.total[h, :, :width] = gn_v[h : h + 1]
    for h in range(heads):
        scores = jnp.where(upper, mm(b_s[rows(h)], a_s[rows(h)], TN), 0.0)
        den_s[h : h + 1] = 1.0 + jnp.sum(scores, axis=0, keepdims=True)
        pt_s[h] = scores.astype(BF16)
    for h in range(heads):
        num_s[rows(h)] = mm(v_v[rows(h)], pt_s[h], NN)
    n_scan.column_send()

    loads[4].wait()
    loads[6].wait()
    for init, state in ((init_s, st_v), (init_r, gs_v)):
        init[...] = jnp.zeros(init.shape, F32)
        for h in range(heads):
            init[tiles(h), :, :width] = state[h].T.reshape(tall, 8, width)
    b_scan.core_rest()
    init_s[...] = init_s[...] + flag(at.c == 1) * b_scan.other[: heads * tall]
    loads[3].wait()
    b_scan.column_send()

    n_scan.finish()
    high, low = split(n_scan.flat[:, :width])
    for h in range(heads):
        both = mm(high, a_s[rows(h)], NN) + mm(low, a_s[rows(h)], NN)
        den_s[h : h + 1] = den_s[h : h + 1] + both[h : h + 1]
    den_s[...] = 1.0 / den_s[...]
    for h in range(heads):
        scaled = g_v[rows(h)].astype(F32) * den_s[h : h + 1]
        ub_s[rows(h)], ul_s[rows(h)] = split(scaled)
    for h in range(heads):
        state = mm(ub_s[rows(h)], a_s[rows(h)], NT)
        c_scan.own[tiles(h), :, :width] = state.reshape(tall, 8, width)
    c_scan.core_send()
    for h in range(heads):
        vp_s[rows(h)] = mm(ub_s[rows(h)], pt_s[h], NT)
    c_scan.plane_send()
    b_scan.back_send()
    c_scan.core_rest()
    init_r[...] = init_r[...] + flag(at.c == 0) * c_scan.other[: heads * tall]
    c_scan.column_send()
    b_scan.back_pass()
    b_scan.finish()

    for h in range(heads):
        state = (b_scan.result[tiles(h)] + init_s[tiles(h)]).reshape(width, LANES)
        sh_s[rows(h)], sl_s[rows(h)] = split(state)
    for h in range(heads):
        numerator = num_s[rows(h)] + mm(sh_s[rows(h), :width], a_s[rows(h)], NN)
        numerator = numerator + mm(sl_s[rows(h), :width], a_s[rows(h)], NN)
        inverse = den_s[h : h + 1]
        scaled = g_v[rows(h)].astype(F32) * inverse
        c_s[h : h + 1] = -jnp.sum(scaled * (numerator * inverse), axis=0, keepdims=True)
    both = jnp.concatenate(split(c_s[...]), axis=0)
    for h in range(heads):
        part = mm(both, a_s[rows(h)], NT)
        m_scan.own[h, :, :width] = part[h : h + 1] + part[16 + h : 17 + h]
    m_scan.core_send()
    m_scan.plane_send()
    c_scan.back_send()

    turned = n_scan.flat[...].T
    for h in range(heads):
        here = rows(h)
        c = c_s[h : h + 1]
        mixed = jnp.where(upper, mm(v_v[here], ub_s[here], TN) + c, 0.0).astype(BF16)
        high, low = sh_s[here, :width], sl_s[here, :width]
        part = mm(high, ub_s[here], TN) + mm(low, ub_s[here], TN) + mm(high, ul_s[here], TN)
        part = part + turned[:width, h : h + 1] * c + mm(b_s[here], mixed, NN)
        dq_v[here] = jnp.where(a_s[here] > 0, part, 0.0).astype(BF16)
        kp_s[here] = mm(a_s[here], mixed, NT)
    m_scan.column_send()
    c_scan.back_pass()
    c_scan.finish()

    for h in range(heads):
        state = (c_scan.result[tiles(h)] + init_r[tiles(h)]).reshape(width, LANES)
        sh_s[rows(h)], sl_s[rows(h)] = split(state)
    for h in range(heads):
        here = rows(h)
        high, low = sh_s[here, :width], sl_s[here, :width]
        part = vp_s[here] + mm(high, b_s[here], NN) + mm(low, b_s[here], NN)
        dv_v[here] = part.astype(BF16)
        kp_s[here] = kp_s[here] + mm(high, v_v[here], TN) + mm(low, v_v[here], TN)
    m_scan.finish()
    turned = m_scan.flat[...].T
    for h in range(heads):
        here = rows(h)
        part = jnp.where(b_s[here] > 0, kp_s[here] + turned[:width, h : h + 1], 0.0)
        dk_v[here] = part.astype(BF16)
    for scan in (n_scan, b_scan, m_scan, c_scan):
        scan.drain()


def small_scratch(groups, chips, heads):
    one = (heads, 1, LANES)
    sem = pltpu.SemaphoreType.DMA
    return [
        pltpu.VMEM(one, F32),
        pltpu.VMEM(one, F32),
        pltpu.VMEM(one, F32),
        pltpu.VMEM((chips, *one), F32),
        pltpu.VMEM((groups, *one), F32),
        pltpu.VMEM(one, F32),
        pltpu.VMEM((16, LANES), F32),
        sem((2, 1)),
        sem((2, chips - 1)),
        sem((2, groups - 1)),
    ]


def large_scratch(groups, chips, share):
    whole = pltpu.VMEM((2 * chips * share, 8, LANES), F32)
    plane = pltpu.VMEM((chips, share, 8, LANES), F32)
    sem = pltpu.SemaphoreType.DMA
    return [
        whole,
        whole,
        plane,
        plane,
        pltpu.VMEM((groups, share, 8, LANES), F32),
        plane,
        whole,
        sem((2, 2)),
        sem((2, chips - 1)),
        sem((2, groups - 1)),
        sem((2, chips - 1)),
        sem((2, chips)),
    ]


def place(*refs):
    sems = refs[6]
    copies = [pltpu.make_async_copy(refs[i], refs[3 + i], sems.at[i]) for i in range(3)]
    for copy in copies:
        copy.start()
    for copy in copies:
        copy.wait()


def per_device(groups, chips, *args):
    args = [x.T for x in args[:4]] + list(args[4:])
    columns, tokens = args[0].shape
    heads, width = args[4].shape[:2]
    share = -(-(heads * width // 8) // (2 * chips))
    token = pltpu.VMEM((columns, tokens), BF16)
    wide = pltpu.VMEM((columns, tokens), F32)
    state = pltpu.VMEM((heads, width, width), F32)
    norm = pltpu.VMEM((heads, width), F32)
    one = pltpu.VMEM((16, tokens), F32)
    init = pltpu.VMEM((heads * width // 8, 8, LANES), F32)
    sem = pltpu.SemaphoreType.DMA
    scratch = [token] * 4 + [state, norm, state, norm]
    scratch += [token] * 4 + [pltpu.VMEM((columns, LANES), BF16)] * 2
    scratch += [pltpu.VMEM((heads, tokens, tokens), BF16)]
    scratch += [wide] * 3 + [one] * 2 + [init] * 2 + [sem((8,))]
    scratch += small_scratch(groups, chips, heads) * 2 + large_scratch(groups, chips, share) * 2
    outs = pl.pallas_call(
        functools.partial(kernel, groups, chips, heads, width, share),
        out_shape=[pltpu.VMEM((columns, tokens), BF16)] * 3,
        in_specs=[pl.BlockSpec(memory_space=pl.ANY)] * 8,
        out_specs=[pl.BlockSpec(memory_space=pltpu.VMEM)] * 3,
        scratch_shapes=scratch,
        compiler_params=pltpu.CompilerParams(
            collective_id=0, has_side_effects=True, vmem_limit_bytes=60 * 2**20
        ),
        name="scan_kernel",
    )(*args)
    outs = pl.pallas_call(
        place,
        out_shape=[jax.ShapeDtypeStruct((columns, tokens), BF16)] * 3,
        in_specs=[pl.BlockSpec(memory_space=pl.ANY)] * 3,
        out_specs=[pl.BlockSpec(memory_space=pl.ANY)] * 3,
        scratch_shapes=[sem((3,))],
        compiler_params=pltpu.CompilerParams(vmem_limit_bytes=2**20),
        name="place_outputs",
    )(*outs)
    return tuple(x.T for x in outs)


def solution(mesh):
    groups, chips = mesh.shape["grp"], mesh.shape["seq"] // 2
    tokens = P(("grp", "seq"), None)
    return jax.shard_map(
        functools.partial(per_device, groups, chips),
        mesh=mesh,
        in_specs=(tokens,) * 4 + (P(),) * 4,
        out_specs=(tokens,) * 3,
        check_vma=False,
    )
```

```python
import functools
import math

import jax
import jax.numpy as jnp
from jax import lax
from jax.experimental import pallas as pl
from jax.experimental.pallas import tpu as pltpu
from jax.sharding import PartitionSpec as P

MESH = pl.DeviceIdType.MESH
F32 = jnp.float32
BF16 = jnp.bfloat16
NN = (((1,), (0,)), ((), ()))
NT = (((1,), (1,)), ((), ()))
TN = (((0,), (0,)), ((), ()))
LANES = 128


def mm(x, y, dims):
    return lax.dot_general(x, y, dims, preferred_element_type=F32)


def split(x):
    high = x.astype(BF16)
    return high, (x - high.astype(F32)).astype(BF16)


class Place:
    def __init__(self, groups, chips):
        self.groups, self.chips = groups, chips
        self.side = math.isqrt(chips)
        self.z = lax.axis_index("grp")
        seq = lax.axis_index("seq")
        self.p, self.c = seq // 2, seq % 2
        self.y, self.x = self.p // self.side, self.p % self.side
        side = self.side
        offsets = [(dy, dx) for dy in range(side) for dx in range(side) if dy or dx]
        self.plane = sorted(offsets, key=lambda o: min(o[0], side - o[0]) + min(o[1], side - o[1]))
        self.column = sorted(range(1, groups), key=lambda d: min(d, groups - d))

    def chip(self, offset, sign):
        side = self.side
        y = (self.y + sign * offset[0] + side) % side
        x = (self.x + sign * offset[1] + side) % side
        return y * side + x

    def plane_to(self, k):
        return self.chip(self.plane[k], 1)

    def plane_from(self, k):
        return self.chip(self.plane[k], -1)

    def z_to(self, k):
        return (self.z + self.column[k]) % self.groups

    def z_from(self, k):
        return (self.z + self.groups - self.column[k]) % self.groups

    def chip_id(self, p):
        return (self.z, p * 2 + self.c)

    def z_id(self, z):
        return (z, self.p * 2 + self.c)

    def core_id(self):
        return (self.z, self.p * 2 + 1 - self.c)


def remote(src, dst, send, recv, device):
    return pltpu.make_async_remote_copy(
        src_ref=src, dst_ref=dst, send_sem=send, recv_sem=recv, device_id=device, device_id_type=MESH
    )


def flag(condition):
    return condition.astype(jnp.int32).astype(F32)


def arrived(ref, sem):
    pltpu.make_async_copy(ref, ref, sem).wait()


def z_send(at, later, start):
    for k in reversed(range(len(at.column))):
        offset = at.column[k]
        target = at.z - offset if later else at.z + offset
        inside = target >= 0 if later else target < at.groups

        @pl.when(inside)
        def _():
            start(target)


def z_arrived(at, below, view, sem):
    for n in range(1, at.groups):

        @pl.when(at.z == (n if below else at.groups - 1 - n))
        def _():
            arrived(view(n), sem)


class SmallScan:
    def __init__(self, at, later, refs):
        self.at, self.later = at, later
        self.own, self.other, self.chip, self.plane, self.column, self.total, self.flat = refs[:7]
        self.sems = refs[7]
        self.reached = (lambda i, me: i > me) if later else (lambda i, me: i < me)

    def core_send(self):
        sems = self.sems
        remote(self.own, self.other, sems.at[0], sems.at[1], self.at.core_id()).start()

    def plane_send(self):
        at, sems = self.at, self.sems
        arrived(self.other, sems.at[1])
        both = self.own[...] + self.other[...]
        self.chip[...] = both
        for k in reversed(range(len(at.plane))):
            device = at.chip_id(at.plane_to(k))
            remote(self.chip, self.plane.at[at.p], sems.at[2], sems.at[3], device).start()
        self.plane[at.p] = both

    def column_send(self):
        at, sems = self.at, self.sems
        arrived(self.plane.at[: at.chips - 1], sems.at[3])
        everything = self.plane[0]
        for p in range(1, at.chips):
            everything = everything + self.plane[p]
        self.column[at.z] = everything
        mine = self.column.at[at.z]
        z_send(
            at,
            self.later,
            lambda z: remote(mine, mine, sems.at[4], sems.at[5], at.z_id(z)).start(),
        )
        near = flag(at.c == (0 if self.later else 1)) * self.other[...]
        for p in range(at.chips):
            near = near + flag(self.reached(p, at.p)) * self.plane[p]
        self.total[...] = self.total[...] + near

    def finish(self):
        at = self.at
        z_arrived(at, not self.later, lambda n: self.column.at[:n], self.sems.at[5])
        far = jnp.where(self.reached(0, at.z), self.column[0], 0.0)
        for z in range(1, at.groups):
            far = far + jnp.where(self.reached(z, at.z), self.column[z], 0.0)
        self.total[...] = self.total[...] + far
        for h in range(self.total.shape[0]):
            self.flat[h : h + 1, :] = self.total[h]

    def drain(self):
        at, sems = self.at, self.sems
        arrived(self.own, sems.at[0])
        arrived(self.plane.at[: at.chips - 1], sems.at[2])
        z_arrived(at, self.later, lambda n: self.column.at[:n], sems.at[4])


class LargeScan:
    def __init__(self, at, later, share, chunks, refs):
        self.at, self.later, self.share, self.chunks = at, later, share, chunks
        self.own, self.other, self.chip, self.plane, self.column, self.back, self.result = refs[:7]
        self.core_s, self.chunk_s, self.back_s = refs[7:]
        self.half = share * at.chips
        self.reached = (lambda i, me: i > me) if later else (lambda i, me: i < me)

    def piece(self, core, p, chunk=None):
        first, count = (0, self.share) if chunk is None else self.chunks[chunk]
        return pl.ds((core * self.at.chips + p) * self.share + first, count)

    def part(self, chunk):
        first, count = self.chunks[chunk]
        return pl.ds(first, count)

    def core_copy(self, k, core):
        half = pl.ds(core * self.half, self.half)
        sems = self.core_s
        return remote(
            self.own.at[half], self.other.at[half], sems.at[0, k], sems.at[1, k], self.at.core_id()
        )

    def core_send(self):
        self.core_copy(0, 1 - self.at.c).start()
        self.core_copy(1, self.at.c).start()

    def core_rest(self):
        self.core_copy(1, 1 - self.at.c).wait_recv()

    def plane_send(self):
        at = self.at
        self.core_copy(0, at.c).wait_recv()
        for i in range(len(self.chunks)):
            part, sems = self.part(i), self.chunk_s.at[i]
            for k in reversed(range(len(at.plane))):
                target = at.plane_to(k)
                piece = self.piece(at.c, target, i)
                self.chip[target, part] = self.own[piece] + self.other[piece]
                remote(
                    self.chip.at[target, part],
                    self.plane.at[at.p, part],
                    sems.at[0],
                    sems.at[1],
                    at.chip_id(target),
                ).start()
        piece = self.piece(at.c, at.p)
        self.plane[at.p] = self.own[piece] + self.other[piece]

    def column_send(self, i):
        at = self.at
        part, sems = self.part(i), self.chunk_s.at[i]
        arrived(self.plane.at[: at.chips - 1, part], sems.at[1])
        order = list(range(at.chips))
        if self.later:
            order.reverse()
        running = jnp.zeros((self.chunks[i][1], *self.column.shape[2:]), F32)
        for p in order:
            self.back[p, part] = running
            running = running + self.plane[p, part]
        self.column[at.z, part] = running
        mine = self.column.at[at.z, part]
        z_send(
            at,
            self.later,
            lambda z: remote(mine, mine, sems.at[2], sems.at[3], at.z_id(z)).start(),
        )

    def pass_on(self, owner):
        mine = self.result.at[self.piece(self.at.c, owner)]
        remote(mine, mine, self.core_s.at[0, 2], self.core_s.at[1, 2], self.at.core_id()).start()

    def back_send(self, i):
        at = self.at
        part, sems = self.part(i), self.chunk_s.at[i]
        z_arrived(at, not self.later, lambda n: self.column.at[:n, part], sems.at[3])
        far = jnp.where(self.reached(0, at.z), self.column[0, part], 0.0)
        for z in range(1, at.groups):
            far = far + jnp.where(self.reached(z, at.z), self.column[z, part], 0.0)
        for k in reversed(range(len(at.plane))):
            target = at.plane_to(k)
            self.back[target, part] = self.back[target, part] + far
            remote(
                self.back.at[target, part],
                self.result.at[self.piece(at.c, at.p, i)],
                sems.at[4],
                self.back_s.at[k],
                at.chip_id(target),
            ).start()
        self.result[self.piece(at.c, at.p, i)] = self.back[at.p, part] + far
        if i == len(self.chunks) - 1:
            self.pass_on(at.p)

    def back_pass(self):
        at = self.at
        for k in range(len(at.plane)):
            source = at.plane_from(k)
            arrived(self.result.at[self.piece(at.c, source)], self.back_s.at[k])
            self.pass_on(source)

    def finish(self):
        half = pl.ds((1 - self.at.c) * self.half, self.half)
        arrived(self.result.at[half], self.core_s.at[1, 2])

    def drain(self):
        at = self.at
        half = pl.ds(0, self.half)
        for k in range(2):
            arrived(self.own.at[half], self.core_s.at[0, k])
        arrived(self.result.at[half], self.core_s.at[0, 2])
        for i in range(len(self.chunks)):
            part, sems = self.part(i), self.chunk_s.at[i]
            arrived(self.plane.at[: at.chips - 1, part], sems.at[0])
            z_arrived(at, self.later, lambda n: self.column.at[:n, part], sems.at[2])
            arrived(self.plane.at[: at.chips - 1, part], sems.at[4])


def kernel(groups, chips, heads, width, share, chunks, *refs):
    hbm_in, (dq_v, dk_v, dv_v), refs = refs[:8], refs[8:11], refs[11:]
    q_v, k_v, v_v, g_v, st_v, nm_v, gs_v, gn_v = refs[:8]
    a_s, b_s, ub_s, ul_s, sh_s, sl_s, pt_s = refs[8:15]
    num_s, kp_s, vp_s, den_s, c_s, init_s, init_r = refs[15:22]
    load_s = refs[22]
    small = refs[23:39]
    large = refs[39:]
    at = Place(groups, chips)
    n_scan = SmallScan(at, False, small[:8])
    m_scan = SmallScan(at, True, small[8:])
    b_scan = LargeScan(at, False, share, chunks, large[:10])
    c_scan = LargeScan(at, True, share, chunks, large[10:])
    tokens = k_v.shape[1]
    tall = width // 8

    loads = [
        pltpu.make_async_copy(src, dst, load_s.at[i])
        for i, (src, dst) in enumerate(zip(hbm_in, (q_v, k_v, v_v, g_v, st_v, nm_v, gs_v, gn_v)))
    ]
    loads[1].start()
    loads[2].start()
    barrier = pltpu.get_barrier_semaphore()
    partners = [at.core_id()]
    partners += [at.chip_id(at.plane_to(k)) for k in range(len(at.plane))]
    partners += [at.z_id(at.z_to(k)) for k in range(len(at.column))]
    for partner in partners:
        pl.semaphore_signal(barrier, inc=1, device_id=partner, device_id_type=MESH)
    for i in (0, 3, 5, 7, 4, 6):
        loads[i].start()

    upper = lax.broadcasted_iota(jnp.int32, (tokens, tokens), 0) <= lax.broadcasted_iota(
        jnp.int32, (tokens, tokens), 1
    )
    for scan in (b_scan, c_scan):
        scan.own[...] = jnp.zeros(scan.own.shape, F32)
    for scan in (n_scan, m_scan):
        scan.own[...] = jnp.zeros(scan.own.shape, F32)
        scan.total[...] = jnp.zeros(scan.total.shape, F32)
        scan.flat[...] = jnp.zeros(scan.flat.shape, F32)
    den_s[...] = jnp.ones(den_s.shape, F32)
    c_s[...] = jnp.zeros(c_s.shape, F32)

    def tiles(h):
        return slice(h * tall, (h + 1) * tall)

    def rows(h):
        return slice(h * width, (h + 1) * width)

    loads[1].wait()
    b_s[...] = jnp.maximum(k_v[...], 0)
    some = jnp.ones((16, tokens), BF16)
    for h in range(heads):
        n_scan.own[h, :, :width] = mm(some, b_s[rows(h)], NT)[0:1]
    pl.semaphore_wait(barrier, len(partners))
    n_scan.core_send()

    loads[2].wait()
    for h in range(heads):
        state = mm(v_v[rows(h)], b_s[rows(h)], NT)
        b_scan.own[tiles(h), :, :width] = state.reshape(tall, 8, width)
    b_scan.core_send()
    n_scan.plane_send()

    loads[0].wait()
    a_s[...] = jnp.maximum(q_v[...], 0)
    b_scan.plane_send()

    loads[5].wait()
    loads[7].wait()
    for h in range(heads):
        n_scan.total[h, :, :width] = nm_v[h : h + 1]
        m_scan.total[h, :, :width] = gn_v[h : h + 1]
    for h in range(heads):
        scores = jnp.where(upper, mm(b_s[rows(h)], a_s[rows(h)], TN), 0.0)
        den_s[h : h + 1] = 1.0 + jnp.sum(scores, axis=0, keepdims=True)
        pt_s[h] = scores.astype(BF16)
    for h in range(heads):
        num_s[rows(h)] = mm(v_v[rows(h)], pt_s[h], NN)
    n_scan.column_send()

    loads[4].wait()
    loads[6].wait()
    for init, state in ((init_s, st_v), (init_r, gs_v)):
        init[...] = jnp.zeros(init.shape, F32)
        for h in range(heads):
            init[tiles(h), :, :width] = state[h].T.reshape(tall, 8, width)
    b_scan.core_rest()
    init_s[...] = init_s[...] + flag(at.c == 1) * b_scan.other[: heads * tall]
    loads[3].wait()
    for i in range(len(chunks)):
        b_scan.column_send(i)

    n_scan.finish()
    high, low = split(n_scan.flat[:, :width])
    for h in range(heads):
        both = mm(high, a_s[rows(h)], NN) + mm(low, a_s[rows(h)], NN)
        den_s[h : h + 1] = den_s[h : h + 1] + both[h : h + 1]
    den_s[...] = 1.0 / den_s[...]
    for h in range(heads):
        scaled = g_v[rows(h)].astype(F32) * den_s[h : h + 1]
        ub_s[rows(h)], ul_s[rows(h)] = split(scaled)
    for h in range(heads):
        state = mm(ub_s[rows(h)], a_s[rows(h)], NT)
        c_scan.own[tiles(h), :, :width] = state.reshape(tall, 8, width)
    c_scan.core_send()
    for h in range(heads):
        vp_s[rows(h)] = mm(ub_s[rows(h)], pt_s[h], NT)
    c_scan.plane_send()
    for i in range(len(chunks)):
        b_scan.back_send(i)
    c_scan.core_rest()
    init_r[...] = init_r[...] + flag(at.c == 0) * c_scan.other[: heads * tall]
    for i in range(len(chunks)):
        c_scan.column_send(i)
    b_scan.back_pass()
    b_scan.finish()

    for h in range(heads):
        state = (b_scan.result[tiles(h)] + init_s[tiles(h)]).reshape(width, LANES)
        sh_s[rows(h)], sl_s[rows(h)] = split(state)
    for h in range(heads):
        numerator = num_s[rows(h)] + mm(sh_s[rows(h), :width], a_s[rows(h)], NN)
        numerator = numerator + mm(sl_s[rows(h), :width], a_s[rows(h)], NN)
        inverse = den_s[h : h + 1]
        scaled = g_v[rows(h)].astype(F32) * inverse
        c_s[h : h + 1] = -jnp.sum(scaled * (numerator * inverse), axis=0, keepdims=True)
    both = jnp.concatenate(split(c_s[...]), axis=0)
    for h in range(heads):
        part = mm(both, a_s[rows(h)], NT)
        m_scan.own[h, :, :width] = part[h : h + 1] + part[16 + h : 17 + h]
    m_scan.core_send()
    m_scan.plane_send()
    for i in range(len(chunks)):
        c_scan.back_send(i)

    turned = n_scan.flat[...].T
    for h in range(heads):
        here = rows(h)
        c = c_s[h : h + 1]
        mixed = jnp.where(upper, mm(v_v[here], ub_s[here], TN) + c, 0.0).astype(BF16)
        high, low = sh_s[here, :width], sl_s[here, :width]
        part = mm(high, ub_s[here], TN) + mm(low, ub_s[here], TN) + mm(high, ul_s[here], TN)
        part = part + turned[:width, h : h + 1] * c + mm(b_s[here], mixed, NN)
        dq_v[here] = jnp.where(a_s[here] > 0, part, 0.0).astype(BF16)
        kp_s[here] = mm(a_s[here], mixed, NT)
    m_scan.column_send()
    c_scan.back_pass()
    c_scan.finish()

    for h in range(heads):
        state = (c_scan.result[tiles(h)] + init_r[tiles(h)]).reshape(width, LANES)
        sh_s[rows(h)], sl_s[rows(h)] = split(state)
    for h in range(heads):
        here = rows(h)
        high, low = sh_s[here, :width], sl_s[here, :width]
        part = vp_s[here] + mm(high, b_s[here], NN) + mm(low, b_s[here], NN)
        dv_v[here] = part.astype(BF16)
        kp_s[here] = kp_s[here] + mm(high, v_v[here], TN) + mm(low, v_v[here], TN)
    m_scan.finish()
    turned = m_scan.flat[...].T
    for h in range(heads):
        here = rows(h)
        part = jnp.where(b_s[here] > 0, kp_s[here] + turned[:width, h : h + 1], 0.0)
        dk_v[here] = part.astype(BF16)
    for scan in (n_scan, b_scan, m_scan, c_scan):
        scan.drain()


def small_scratch(groups, chips, heads):
    one = (heads, 1, LANES)
    return [
        pltpu.VMEM(one, F32),
        pltpu.VMEM(one, F32),
        pltpu.VMEM(one, F32),
        pltpu.VMEM((chips, *one), F32),
        pltpu.VMEM((groups, *one), F32),
        pltpu.VMEM(one, F32),
        pltpu.VMEM((16, LANES), F32),
        pltpu.SemaphoreType.DMA((6,)),
    ]


def large_scratch(groups, chips, share, chunks):
    whole = pltpu.VMEM((2 * chips * share, 8, LANES), F32)
    plane = pltpu.VMEM((chips, share, 8, LANES), F32)
    sem = pltpu.SemaphoreType.DMA
    return [
        whole,
        whole,
        plane,
        plane,
        pltpu.VMEM((groups, share, 8, LANES), F32),
        plane,
        whole,
        sem((2, 3)),
        sem((len(chunks), 5)),
        sem((chips - 1,)),
    ]


def place(*refs):
    sems = refs[6]
    copies = [pltpu.make_async_copy(refs[i], refs[3 + i], sems.at[i]) for i in range(3)]
    for copy in copies:
        copy.start()
    for copy in copies:
        copy.wait()


def per_device(groups, chips, *args):
    args = [x.T for x in args[:4]] + list(args[4:])
    columns, tokens = args[0].shape
    heads, width = args[4].shape[:2]
    share = -(-(heads * width // 8) // (2 * chips))
    chunks = ((0, share),)
    token = pltpu.VMEM((columns, tokens), BF16)
    wide = pltpu.VMEM((columns, tokens), F32)
    state = pltpu.VMEM((heads, width, width), F32)
    norm = pltpu.VMEM((heads, width), F32)
    one = pltpu.VMEM((16, tokens), F32)
    init = pltpu.VMEM((heads * width // 8, 8, LANES), F32)
    sem = pltpu.SemaphoreType.DMA
    scratch = [token] * 4 + [state, norm, state, norm]
    scratch += [token] * 4 + [pltpu.VMEM((columns, LANES), BF16)] * 2
    scratch += [pltpu.VMEM((heads, tokens, tokens), BF16)]
    scratch += [wide] * 3 + [one] * 2 + [init] * 2 + [sem((8,))]
    scratch += small_scratch(groups, chips, heads) * 2 + large_scratch(groups, chips, share, chunks) * 2
    outs = pl.pallas_call(
        functools.partial(kernel, groups, chips, heads, width, share, chunks),
        out_shape=[pltpu.VMEM((columns, tokens), BF16)] * 3,
        in_specs=[pl.BlockSpec(memory_space=pl.ANY)] * 8,
        out_specs=[pl.BlockSpec(memory_space=pltpu.VMEM)] * 3,
        scratch_shapes=scratch,
        compiler_params=pltpu.CompilerParams(
            collective_id=0, has_side_effects=True, vmem_limit_bytes=60 * 2**20
        ),
        name="scan_kernel",
    )(*args)
    outs = pl.pallas_call(
        place,
        out_shape=[jax.ShapeDtypeStruct((columns, tokens), BF16)] * 3,
        in_specs=[pl.BlockSpec(memory_space=pl.ANY)] * 3,
        out_specs=[pl.BlockSpec(memory_space=pl.ANY)] * 3,
        scratch_shapes=[sem((3,))],
        compiler_params=pltpu.CompilerParams(vmem_limit_bytes=2**20),
        name="place_outputs",
    )(*outs)
    return tuple(x.T for x in outs)


def solution(mesh):
    groups, chips = mesh.shape["grp"], mesh.shape["seq"] // 2
    tokens = P(("grp", "seq"), None)
    return jax.shard_map(
        functools.partial(per_device, groups, chips),
        mesh=mesh,
        in_specs=(tokens,) * 4 + (P(),) * 4,
        out_specs=(tokens,) * 3,
        check_vma=False,
    )
```

```python
import functools
import math

import jax
import jax.numpy as jnp
from jax import lax
from jax.experimental import pallas as pl
from jax.experimental.pallas import tpu as pltpu
from jax.sharding import PartitionSpec as P

MESH = pl.DeviceIdType.MESH
F32 = jnp.float32
BF16 = jnp.bfloat16
NN = (((1,), (0,)), ((), ()))
NT = (((1,), (1,)), ((), ()))
TN = (((0,), (0,)), ((), ()))
LANES = 128


def mm(x, y, dims):
    return lax.dot_general(x, y, dims, preferred_element_type=F32)


def split(x):
    high = x.astype(BF16)
    return high, (x - high.astype(F32)).astype(BF16)


class Place:
    def __init__(self, groups, chips):
        self.groups, self.chips = groups, chips
        self.side = math.isqrt(chips)
        self.z = lax.axis_index("grp")
        seq = lax.axis_index("seq")
        self.p, self.c = seq // 2, seq % 2
        self.y, self.x = self.p // self.side, self.p % self.side
        side = self.side
        offsets = [(dy, dx) for dy in range(side) for dx in range(side) if dy or dx]
        self.plane = sorted(offsets, key=lambda o: min(o[0], side - o[0]) + min(o[1], side - o[1]))
        self.column = sorted(range(1, groups), key=lambda d: min(d, groups - d))

    def chip(self, offset, sign):
        side = self.side
        y = (self.y + sign * offset[0] + side) % side
        x = (self.x + sign * offset[1] + side) % side
        return y * side + x

    def plane_to(self, k):
        return self.chip(self.plane[k], 1)

    def plane_from(self, k):
        return self.chip(self.plane[k], -1)

    def z_to(self, k):
        return (self.z + self.column[k]) % self.groups

    def z_from(self, k):
        return (self.z + self.groups - self.column[k]) % self.groups

    def chip_id(self, p):
        return (self.z, p * 2 + self.c)

    def z_id(self, z):
        return (z, self.p * 2 + self.c)

    def core_id(self):
        return (self.z, self.p * 2 + 1 - self.c)


def remote(src, dst, send, recv, device):
    return pltpu.make_async_remote_copy(
        src_ref=src, dst_ref=dst, send_sem=send, recv_sem=recv, device_id=device, device_id_type=MESH
    )


def flag(condition):
    return condition.astype(jnp.int32).astype(F32)


def arrived(ref, sem):
    pltpu.make_async_copy(ref, ref, sem).wait()


def z_send(at, later, start):
    for k in reversed(range(len(at.column))):
        offset = at.column[k]
        target = at.z - offset if later else at.z + offset
        inside = target >= 0 if later else target < at.groups

        @pl.when(inside)
        def _():
            start(target)


def z_arrived(at, below, view, sem):
    for n in range(1, at.groups):

        @pl.when(at.z == (n if below else at.groups - 1 - n))
        def _():
            arrived(view(n), sem)


class SmallScan:
    def __init__(self, at, later, refs):
        self.at, self.later = at, later
        self.own, self.other, self.chip, self.plane, self.column, self.total, self.flat = refs[:7]
        self.sems = refs[7]
        self.reached = (lambda i, me: i > me) if later else (lambda i, me: i < me)

    def core_send(self):
        sems = self.sems
        remote(self.own, self.other, sems.at[0], sems.at[1], self.at.core_id()).start()

    def plane_send(self):
        at, sems = self.at, self.sems
        arrived(self.other, sems.at[1])
        both = self.own[...] + self.other[...]
        self.chip[...] = both
        for k in reversed(range(len(at.plane))):
            device = at.chip_id(at.plane_to(k))
            remote(self.chip, self.plane.at[at.p], sems.at[2], sems.at[3], device).start()
        self.plane[at.p] = both

    def column_send(self):
        at, sems = self.at, self.sems
        arrived(self.plane.at[: at.chips - 1], sems.at[3])
        everything = self.plane[0]
        for p in range(1, at.chips):
            everything = everything + self.plane[p]
        self.column[at.z] = everything
        mine = self.column.at[at.z]
        z_send(
            at,
            self.later,
            lambda z: remote(mine, mine, sems.at[4], sems.at[5], at.z_id(z)).start(),
        )
        near = flag(at.c == (0 if self.later else 1)) * self.other[...]
        for p in range(at.chips):
            near = near + flag(self.reached(p, at.p)) * self.plane[p]
        self.total[...] = self.total[...] + near

    def finish(self):
        at = self.at
        z_arrived(at, not self.later, lambda n: self.column.at[:n], self.sems.at[5])
        far = jnp.where(self.reached(0, at.z), self.column[0], 0.0)
        for z in range(1, at.groups):
            far = far + jnp.where(self.reached(z, at.z), self.column[z], 0.0)
        self.total[...] = self.total[...] + far
        for h in range(self.total.shape[0]):
            self.flat[h : h + 1, :] = self.total[h]

    def drain(self):
        at, sems = self.at, self.sems
        arrived(self.own, sems.at[0])
        arrived(self.plane.at[: at.chips - 1], sems.at[2])
        z_arrived(at, self.later, lambda n: self.column.at[:n], sems.at[4])


class LargeScan:
    def __init__(self, at, later, share, chunks, refs):
        self.at, self.later, self.share, self.chunks = at, later, share, chunks
        self.own, self.other, self.chip, self.plane, self.column, self.back, self.result = refs[:7]
        self.core_s, self.chunk_s, self.back_s = refs[7:]
        self.half = share * at.chips
        self.reached = (lambda i, me: i > me) if later else (lambda i, me: i < me)

    def piece(self, core, p, chunk=None):
        first, count = (0, self.share) if chunk is None else self.chunks[chunk]
        return pl.ds((core * self.at.chips + p) * self.share + first, count)

    def part(self, chunk):
        first, count = self.chunks[chunk]
        return pl.ds(first, count)

    def core_copy(self, k, core):
        half = pl.ds(core * self.half, self.half)
        sems = self.core_s
        return remote(
            self.own.at[half], self.other.at[half], sems.at[0, k], sems.at[1, k], self.at.core_id()
        )

    def core_send(self):
        self.core_copy(0, 1 - self.at.c).start()

    def core_rest(self):
        self.core_copy(1, 1 - self.at.c).wait_recv()

    def plane_send(self):
        at = self.at
        self.core_copy(0, at.c).wait_recv()
        for i in range(len(self.chunks)):
            part, sems = self.part(i), self.chunk_s.at[i]
            for k in reversed(range(len(at.plane))):
                target = at.plane_to(k)
                piece = self.piece(at.c, target, i)
                self.chip[target, part] = self.own[piece] + self.other[piece]
                remote(
                    self.chip.at[target, part],
                    self.plane.at[at.p, part],
                    sems.at[0],
                    sems.at[1],
                    at.chip_id(target),
                ).start()
        self.core_copy(1, at.c).start()
        piece = self.piece(at.c, at.p)
        self.plane[at.p] = self.own[piece] + self.other[piece]

    def column_send(self, i):
        at = self.at
        part, sems = self.part(i), self.chunk_s.at[i]
        arrived(self.plane.at[: at.chips - 1, part], sems.at[1])
        order = list(range(at.chips))
        if self.later:
            order.reverse()
        running = jnp.zeros((self.chunks[i][1], *self.column.shape[2:]), F32)
        for p in order:
            self.back[p, part] = running
            running = running + self.plane[p, part]
        self.column[at.z, part] = running
        mine = self.column.at[at.z, part]
        z_send(
            at,
            self.later,
            lambda z: remote(mine, mine, sems.at[2], sems.at[3], at.z_id(z)).start(),
        )

    def pass_on(self, owner):
        mine = self.result.at[self.piece(self.at.c, owner)]
        remote(mine, mine, self.core_s.at[0, 2], self.core_s.at[1, 2], self.at.core_id()).start()

    def back_send(self, i):
        at = self.at
        part, sems = self.part(i), self.chunk_s.at[i]
        z_arrived(at, not self.later, lambda n: self.column.at[:n, part], sems.at[3])
        far = jnp.where(self.reached(0, at.z), self.column[0, part], 0.0)
        for z in range(1, at.groups):
            far = far + jnp.where(self.reached(z, at.z), self.column[z, part], 0.0)
        for k in reversed(range(len(at.plane))):
            target = at.plane_to(k)
            self.back[target, part] = self.back[target, part] + far
            remote(
                self.back.at[target, part],
                self.result.at[self.piece(at.c, at.p, i)],
                sems.at[4],
                self.back_s.at[k],
                at.chip_id(target),
            ).start()
        self.result[self.piece(at.c, at.p, i)] = self.back[at.p, part] + far
        if i == len(self.chunks) - 1:
            self.pass_on(at.p)

    def back_pass(self):
        at = self.at
        for k in range(len(at.plane)):
            source = at.plane_from(k)
            arrived(self.result.at[self.piece(at.c, source)], self.back_s.at[k])
            self.pass_on(source)

    def finish(self):
        half = pl.ds((1 - self.at.c) * self.half, self.half)
        arrived(self.result.at[half], self.core_s.at[1, 2])

    def drain(self):
        at = self.at
        half = pl.ds(0, self.half)
        for k in range(2):
            arrived(self.own.at[half], self.core_s.at[0, k])
        arrived(self.result.at[half], self.core_s.at[0, 2])
        for i in range(len(self.chunks)):
            part, sems = self.part(i), self.chunk_s.at[i]
            arrived(self.plane.at[: at.chips - 1, part], sems.at[0])
            z_arrived(at, self.later, lambda n: self.column.at[:n, part], sems.at[2])
            arrived(self.plane.at[: at.chips - 1, part], sems.at[4])


def kernel(groups, chips, heads, width, share, chunks, *refs):
    hbm_in, (dq_v, dk_v, dv_v), refs = refs[:8], refs[8:11], refs[11:]
    q_v, k_v, v_v, g_v, st_v, nm_v, gs_v, gn_v = refs[:8]
    a_s, b_s, ub_s, ul_s, sh_s, sl_s, pt_s = refs[8:15]
    num_s, kp_s, vp_s, den_s, c_s, init_s, init_r = refs[15:22]
    load_s = refs[22]
    small = refs[23:39]
    large = refs[39:]
    at = Place(groups, chips)
    n_scan = SmallScan(at, False, small[:8])
    m_scan = SmallScan(at, True, small[8:])
    b_scan = LargeScan(at, False, share, chunks, large[:10])
    c_scan = LargeScan(at, True, share, chunks, large[10:])
    tokens = k_v.shape[1]
    tall = width // 8

    loads = [
        pltpu.make_async_copy(src, dst, load_s.at[i])
        for i, (src, dst) in enumerate(zip(hbm_in, (q_v, k_v, v_v, g_v, st_v, nm_v, gs_v, gn_v)))
    ]
    loads[1].start()
    loads[2].start()
    barrier = pltpu.get_barrier_semaphore()
    partners = [at.core_id()]
    partners += [at.chip_id(at.plane_to(k)) for k in range(len(at.plane))]
    partners += [at.z_id(at.z_to(k)) for k in range(len(at.column))]
    for partner in partners:
        pl.semaphore_signal(barrier, inc=1, device_id=partner, device_id_type=MESH)
    for i in (0, 3, 5, 7, 4, 6):
        loads[i].start()

    upper = lax.broadcasted_iota(jnp.int32, (tokens, tokens), 0) <= lax.broadcasted_iota(
        jnp.int32, (tokens, tokens), 1
    )
    for scan in (b_scan, c_scan):
        scan.own[...] = jnp.zeros(scan.own.shape, F32)
    for scan in (n_scan, m_scan):
        scan.own[...] = jnp.zeros(scan.own.shape, F32)
        scan.total[...] = jnp.zeros(scan.total.shape, F32)
        scan.flat[...] = jnp.zeros(scan.flat.shape, F32)
    den_s[...] = jnp.ones(den_s.shape, F32)
    c_s[...] = jnp.zeros(c_s.shape, F32)

    def tiles(h):
        return slice(h * tall, (h + 1) * tall)

    def rows(h):
        return slice(h * width, (h + 1) * width)

    loads[1].wait()
    b_s[...] = jnp.maximum(k_v[...], 0)
    some = jnp.ones((16, tokens), BF16)
    for h in range(heads):
        n_scan.own[h, :, :width] = mm(some, b_s[rows(h)], NT)[0:1]
    pl.semaphore_wait(barrier, len(partners))
    n_scan.core_send()

    loads[2].wait()
    for h in range(heads):
        state = mm(v_v[rows(h)], b_s[rows(h)], NT)
        b_scan.own[tiles(h), :, :width] = state.reshape(tall, 8, width)
    n_scan.plane_send()
    b_scan.core_send()

    loads[0].wait()
    a_s[...] = jnp.maximum(q_v[...], 0)
    b_scan.plane_send()

    loads[5].wait()
    loads[7].wait()
    for h in range(heads):
        n_scan.total[h, :, :width] = nm_v[h : h + 1]
        m_scan.total[h, :, :width] = gn_v[h : h + 1]
    for h in range(heads):
        scores = jnp.where(upper, mm(b_s[rows(h)], a_s[rows(h)], TN), 0.0)
        den_s[h : h + 1] = 1.0 + jnp.sum(scores, axis=0, keepdims=True)
        pt_s[h] = scores.astype(BF16)
    for h in range(heads):
        num_s[rows(h)] = mm(v_v[rows(h)], pt_s[h], NN)
    n_scan.column_send()

    loads[4].wait()
    loads[6].wait()
    for init, state in ((init_s, st_v), (init_r, gs_v)):
        init[...] = jnp.zeros(init.shape, F32)
        for h in range(heads):
            init[tiles(h), :, :width] = state[h].T.reshape(tall, 8, width)
    b_scan.core_rest()
    init_s[...] = init_s[...] + flag(at.c == 1) * b_scan.other[: heads * tall]
    loads[3].wait()

    n_scan.finish()
    high, low = split(n_scan.flat[:, :width])
    for h in range(heads):
        both = mm(high, a_s[rows(h)], NN) + mm(low, a_s[rows(h)], NN)
        den_s[h : h + 1] = den_s[h : h + 1] + both[h : h + 1]
    den_s[...] = 1.0 / den_s[...]
    for h in range(heads):
        scaled = g_v[rows(h)].astype(F32) * den_s[h : h + 1]
        ub_s[rows(h)], ul_s[rows(h)] = split(scaled)
    for h in range(heads):
        state = mm(ub_s[rows(h)], a_s[rows(h)], NT)
        c_scan.own[tiles(h), :, :width] = state.reshape(tall, 8, width)
    c_scan.core_send()
    for i in range(len(chunks)):
        b_scan.column_send(i)
    for h in range(heads):
        vp_s[rows(h)] = mm(ub_s[rows(h)], pt_s[h], NT)
    c_scan.plane_send()
    for i in range(len(chunks)):
        b_scan.back_send(i)
    c_scan.core_rest()
    init_r[...] = init_r[...] + flag(at.c == 0) * c_scan.other[: heads * tall]
    for i in range(len(chunks)):
        c_scan.column_send(i)
    b_scan.back_pass()
    b_scan.finish()

    for h in range(heads):
        state = (b_scan.result[tiles(h)] + init_s[tiles(h)]).reshape(width, LANES)
        sh_s[rows(h)], sl_s[rows(h)] = split(state)
    for h in range(heads):
        numerator = num_s[rows(h)] + mm(sh_s[rows(h), :width], a_s[rows(h)], NN)
        numerator = numerator + mm(sl_s[rows(h), :width], a_s[rows(h)], NN)
        inverse = den_s[h : h + 1]
        scaled = g_v[rows(h)].astype(F32) * inverse
        c_s[h : h + 1] = -jnp.sum(scaled * (numerator * inverse), axis=0, keepdims=True)
    both = jnp.concatenate(split(c_s[...]), axis=0)
    for h in range(heads):
        part = mm(both, a_s[rows(h)], NT)
        m_scan.own[h, :, :width] = part[h : h + 1] + part[16 + h : 17 + h]
    m_scan.core_send()
    m_scan.plane_send()
    for i in range(len(chunks)):
        c_scan.back_send(i)

    turned = n_scan.flat[...].T
    for h in range(heads):
        here = rows(h)
        c = c_s[h : h + 1]
        mixed = jnp.where(upper, mm(v_v[here], ub_s[here], TN) + c, 0.0).astype(BF16)
        high, low = sh_s[here, :width], sl_s[here, :width]
        part = mm(high, ub_s[here], TN) + mm(low, ub_s[here], TN) + mm(high, ul_s[here], TN)
        part = part + turned[:width, h : h + 1] * c + mm(b_s[here], mixed, NN)
        dq_v[here] = jnp.where(a_s[here] > 0, part, 0.0).astype(BF16)
        kp_s[here] = mm(a_s[here], mixed, NT)
    m_scan.column_send()
    c_scan.back_pass()
    c_scan.finish()

    for h in range(heads):
        state = (c_scan.result[tiles(h)] + init_r[tiles(h)]).reshape(width, LANES)
        sh_s[rows(h)], sl_s[rows(h)] = split(state)
    for h in range(heads):
        here = rows(h)
        high, low = sh_s[here, :width], sl_s[here, :width]
        part = vp_s[here] + mm(high, b_s[here], NN) + mm(low, b_s[here], NN)
        dv_v[here] = part.astype(BF16)
        kp_s[here] = kp_s[here] + mm(high, v_v[here], TN) + mm(low, v_v[here], TN)
    m_scan.finish()
    turned = m_scan.flat[...].T
    for h in range(heads):
        here = rows(h)
        part = jnp.where(b_s[here] > 0, kp_s[here] + turned[:width, h : h + 1], 0.0)
        dk_v[here] = part.astype(BF16)
    for scan in (n_scan, b_scan, m_scan, c_scan):
        scan.drain()


def small_scratch(groups, chips, heads):
    one = (heads, 1, LANES)
    return [
        pltpu.VMEM(one, F32),
        pltpu.VMEM(one, F32),
        pltpu.VMEM(one, F32),
        pltpu.VMEM((chips, *one), F32),
        pltpu.VMEM((groups, *one), F32),
        pltpu.VMEM(one, F32),
        pltpu.VMEM((16, LANES), F32),
        pltpu.SemaphoreType.DMA((6,)),
    ]


def large_scratch(groups, chips, share, chunks):
    whole = pltpu.VMEM((2 * chips * share, 8, LANES), F32)
    plane = pltpu.VMEM((chips, share, 8, LANES), F32)
    sem = pltpu.SemaphoreType.DMA
    return [
        whole,
        whole,
        plane,
        plane,
        pltpu.VMEM((groups, share, 8, LANES), F32),
        plane,
        whole,
        sem((2, 3)),
        sem((len(chunks), 5)),
        sem((chips - 1,)),
    ]


def place(*refs):
    sems = refs[6]
    copies = [pltpu.make_async_copy(refs[i], refs[3 + i], sems.at[i]) for i in range(3)]
    for copy in copies:
        copy.start()
    for copy in copies:
        copy.wait()


def per_device(groups, chips, *args):
    args = [x.T for x in args[:4]] + list(args[4:])
    columns, tokens = args[0].shape
    heads, width = args[4].shape[:2]
    share = -(-(heads * width // 8) // (2 * chips))
    chunks = ((0, share),)
    token = pltpu.VMEM((columns, tokens), BF16)
    wide = pltpu.VMEM((columns, tokens), F32)
    state = pltpu.VMEM((heads, width, width), F32)
    norm = pltpu.VMEM((heads, width), F32)
    one = pltpu.VMEM((16, tokens), F32)
    init = pltpu.VMEM((heads * width // 8, 8, LANES), F32)
    sem = pltpu.SemaphoreType.DMA
    scratch = [token] * 4 + [state, norm, state, norm]
    scratch += [token] * 4 + [pltpu.VMEM((columns, LANES), BF16)] * 2
    scratch += [pltpu.VMEM((heads, tokens, tokens), BF16)]
    scratch += [wide] * 3 + [one] * 2 + [init] * 2 + [sem((8,))]
    scratch += small_scratch(groups, chips, heads) * 2 + large_scratch(groups, chips, share, chunks) * 2
    outs = pl.pallas_call(
        functools.partial(kernel, groups, chips, heads, width, share, chunks),
        out_shape=[pltpu.VMEM((columns, tokens), BF16)] * 3,
        in_specs=[pl.BlockSpec(memory_space=pl.ANY)] * 8,
        out_specs=[pl.BlockSpec(memory_space=pltpu.VMEM)] * 3,
        scratch_shapes=scratch,
        compiler_params=pltpu.CompilerParams(
            collective_id=0, has_side_effects=True, vmem_limit_bytes=60 * 2**20
        ),
        name="scan_kernel",
    )(*args)
    outs = pl.pallas_call(
        place,
        out_shape=[jax.ShapeDtypeStruct((columns, tokens), BF16)] * 3,
        in_specs=[pl.BlockSpec(memory_space=pl.ANY)] * 3,
        out_specs=[pl.BlockSpec(memory_space=pl.ANY)] * 3,
        scratch_shapes=[sem((3,))],
        compiler_params=pltpu.CompilerParams(vmem_limit_bytes=2**20),
        name="place_outputs",
    )(*outs)
    return tuple(x.T for x in outs)


def solution(mesh):
    groups, chips = mesh.shape["grp"], mesh.shape["seq"] // 2
    tokens = P(("grp", "seq"), None)
    return jax.shard_map(
        functools.partial(per_device, groups, chips),
        mesh=mesh,
        in_specs=(tokens,) * 4 + (P(),) * 4,
        out_specs=(tokens,) * 3,
        check_vma=False,
    )
```

```python
import functools
import math

import jax
import jax.numpy as jnp
from jax import lax
from jax.experimental import pallas as pl
from jax.experimental.pallas import tpu as pltpu
from jax.sharding import PartitionSpec as P

MESH = pl.DeviceIdType.MESH
F32 = jnp.float32
BF16 = jnp.bfloat16
NN = (((1,), (0,)), ((), ()))
NT = (((1,), (1,)), ((), ()))
TN = (((0,), (0,)), ((), ()))
LANES = 128


def mm(x, y, dims):
    return lax.dot_general(x, y, dims, preferred_element_type=F32)


def split(x):
    high = x.astype(BF16)
    return high, (x - high.astype(F32)).astype(BF16)


class Place:
    def __init__(self, groups, chips):
        self.groups, self.chips = groups, chips
        self.side = math.isqrt(chips)
        self.z = lax.axis_index("grp")
        seq = lax.axis_index("seq")
        self.p, self.c = seq // 2, seq % 2
        self.y, self.x = self.p // self.side, self.p % self.side
        side = self.side
        offsets = [(dy, dx) for dy in range(side) for dx in range(side) if dy or dx]
        self.plane = sorted(offsets, key=lambda o: min(o[0], side - o[0]) + min(o[1], side - o[1]))
        self.far_rows = sorted(range(side), key=lambda d: -min(d, side - d))
        self.column = sorted(range(1, groups), key=lambda d: min(d, groups - d))

    def chip(self, offset, sign):
        side = self.side
        y = (self.y + sign * offset[0] + side) % side
        x = (self.x + sign * offset[1] + side) % side
        return y * side + x

    def plane_to(self, k):
        return self.chip(self.plane[k], 1)

    def plane_from(self, k):
        return self.chip(self.plane[k], -1)

    def z_to(self, k):
        return (self.z + self.column[k]) % self.groups

    def z_from(self, k):
        return (self.z + self.groups - self.column[k]) % self.groups

    def chip_id(self, p):
        return (self.z, p * 2 + self.c)

    def z_id(self, z):
        return (z, self.p * 2 + self.c)

    def core_id(self):
        return (self.z, self.p * 2 + 1 - self.c)


def remote(src, dst, send, recv, device):
    return pltpu.make_async_remote_copy(
        src_ref=src, dst_ref=dst, send_sem=send, recv_sem=recv, device_id=device, device_id_type=MESH
    )


def flag(condition):
    return condition.astype(jnp.int32).astype(F32)


def arrived(ref, sem):
    pltpu.make_async_copy(ref, ref, sem).wait()


def z_send(at, later, start):
    for k in reversed(range(len(at.column))):
        offset = at.column[k]
        target = at.z - offset if later else at.z + offset
        inside = target >= 0 if later else target < at.groups

        @pl.when(inside)
        def _():
            start(target)


def z_arrived(at, below, view, sem):
    for n in range(1, at.groups):

        @pl.when(at.z == (n if below else at.groups - 1 - n))
        def _():
            arrived(view(n), sem)


class SmallScan:
    def __init__(self, at, later, refs):
        self.at, self.later = at, later
        self.own, self.other, self.chip, self.plane, self.column, self.total, self.flat = refs[:7]
        self.sems = refs[7]
        self.reached = (lambda i, me: i > me) if later else (lambda i, me: i < me)

    def core_send(self):
        sems = self.sems
        remote(self.own, self.other, sems.at[0], sems.at[1], self.at.core_id()).start()

    def plane_send(self):
        at, sems = self.at, self.sems
        arrived(self.other, sems.at[1])
        both = self.own[...] + self.other[...]
        self.chip[...] = both
        for k in reversed(range(len(at.plane))):
            device = at.chip_id(at.plane_to(k))
            remote(self.chip, self.plane.at[at.p], sems.at[2], sems.at[3], device).start()
        self.plane[at.p] = both

    def column_send(self):
        at, sems = self.at, self.sems
        arrived(self.plane.at[: at.chips - 1], sems.at[3])
        everything = self.plane[0]
        for p in range(1, at.chips):
            everything = everything + self.plane[p]
        self.column[at.z] = everything
        mine = self.column.at[at.z]
        z_send(
            at,
            self.later,
            lambda z: remote(mine, mine, sems.at[4], sems.at[5], at.z_id(z)).start(),
        )
        near = flag(at.c == (0 if self.later else 1)) * self.other[...]
        for p in range(at.chips):
            near = near + flag(self.reached(p, at.p)) * self.plane[p]
        self.total[...] = self.total[...] + near

    def finish(self):
        at = self.at
        z_arrived(at, not self.later, lambda n: self.column.at[:n], self.sems.at[5])
        far = jnp.where(self.reached(0, at.z), self.column[0], 0.0)
        for z in range(1, at.groups):
            far = far + jnp.where(self.reached(z, at.z), self.column[z], 0.0)
        self.total[...] = self.total[...] + far
        for h in range(self.total.shape[0]):
            self.flat[h : h + 1, :] = self.total[h]

    def drain(self):
        at, sems = self.at, self.sems
        arrived(self.own, sems.at[0])
        arrived(self.plane.at[: at.chips - 1], sems.at[2])
        z_arrived(at, self.later, lambda n: self.column.at[:n], sems.at[4])


class LargeScan:
    def __init__(self, at, later, share, chunks, refs):
        self.at, self.later, self.share, self.chunks = at, later, share, chunks
        self.own, self.other, self.chip, self.plane, self.column, self.back, self.result = refs[:7]
        self.core_s, self.chunk_s, self.back_s = refs[7:]
        self.half = share * at.chips
        self.reached = (lambda i, me: i > me) if later else (lambda i, me: i < me)

    def piece(self, core, p, chunk=None):
        first, count = (0, self.share) if chunk is None else self.chunks[chunk]
        return pl.ds((core * self.at.chips + p) * self.share + first, count)

    def part(self, chunk):
        first, count = self.chunks[chunk]
        return pl.ds(first, count)

    def core_copy(self, k, core):
        half = pl.ds(core * self.half, self.half)
        sems = self.core_s
        return remote(
            self.own.at[half], self.other.at[half], sems.at[0, k], sems.at[1, k], self.at.core_id()
        )

    def core_send(self):
        self.core_copy(0, 1 - self.at.c).start()

    def core_rest(self):
        self.core_copy(1, 1 - self.at.c).wait_recv()

    def plane_send(self):
        at = self.at
        self.core_copy(0, at.c).wait_recv()
        for i in range(len(self.chunks)):
            part, sems = self.part(i), self.chunk_s.at[i]
            for k in reversed(range(len(at.plane))):
                target = at.plane_to(k)
                piece = self.piece(at.c, target, i)
                self.chip[target, part] = self.own[piece] + self.other[piece]
                remote(
                    self.chip.at[target, part],
                    self.plane.at[at.p, part],
                    sems.at[0],
                    sems.at[1],
                    at.chip_id(target),
                ).start()
        self.core_copy(1, at.c).start()
        piece = self.piece(at.c, at.p)
        self.plane[at.p] = self.own[piece] + self.other[piece]

    def column_send(self, i):
        at = self.at
        part, sems = self.part(i), self.chunk_s.at[i]
        arrived(self.plane.at[: at.chips - 1, part], sems.at[1])
        order = list(range(at.chips))
        if self.later:
            order.reverse()
        running = jnp.zeros((self.chunks[i][1], *self.column.shape[2:]), F32)
        for p in order:
            self.back[p, part] = running
            running = running + self.plane[p, part]
        self.column[at.z, part] = running
        mine = self.column.at[at.z, part]
        z_send(
            at,
            self.later,
            lambda z: remote(mine, mine, sems.at[2], sems.at[3], at.z_id(z)).start(),
        )

    def back_send(self, i):
        at = self.at
        part, sems = self.part(i), self.chunk_s.at[i]
        z_arrived(at, not self.later, lambda n: self.column.at[:n, part], sems.at[3])
        far = jnp.where(self.reached(0, at.z), self.column[0, part], 0.0)
        for z in range(1, at.groups):
            far = far + jnp.where(self.reached(z, at.z), self.column[z, part], 0.0)
        for k in reversed(range(len(at.plane))):
            target = at.plane_to(k)
            self.back[target, part] = self.back[target, part] + far
            remote(
                self.back.at[target, part],
                self.result.at[self.piece(at.c, at.p, i)],
                sems.at[4],
                self.back_s.at[at.plane[k][0]],
                at.chip_id(target),
            ).start()
        self.result[self.piece(at.c, at.p, i)] = self.back[at.p, part] + far

    def back_pass(self):
        at = self.at
        for dy in reversed(at.far_rows):
            first = at.c * at.chips + (at.y + at.side - dy) % at.side * at.side
            row = self.result.at[pl.ds(first * self.share, at.side * self.share)]
            count = at.side if dy else at.side - 1
            arrived(self.result.at[pl.ds(first * self.share, count * self.share)], self.back_s.at[dy])
            remote(row, row, self.core_s.at[0, 2], self.core_s.at[1, 2], at.core_id()).start()

    def finish(self):
        half = pl.ds((1 - self.at.c) * self.half, self.half)
        arrived(self.result.at[half], self.core_s.at[1, 2])

    def drain(self):
        at = self.at
        half = pl.ds(0, self.half)
        for k in range(2):
            arrived(self.own.at[half], self.core_s.at[0, k])
        arrived(self.result.at[half], self.core_s.at[0, 2])
        for i in range(len(self.chunks)):
            part, sems = self.part(i), self.chunk_s.at[i]
            arrived(self.plane.at[: at.chips - 1, part], sems.at[0])
            z_arrived(at, self.later, lambda n: self.column.at[:n, part], sems.at[2])
            arrived(self.plane.at[: at.chips - 1, part], sems.at[4])


def kernel(groups, chips, heads, width, share, chunks, *refs):
    hbm_in, (dq_v, dk_v, dv_v), refs = refs[:8], refs[8:11], refs[11:]
    q_v, k_v, v_v, g_v, st_v, nm_v, gs_v, gn_v = refs[:8]
    a_s, b_s, ub_s, ul_s, sh_s, sl_s, pt_s = refs[8:15]
    num_s, kp_s, vp_s, den_s, c_s, init_s, init_r = refs[15:22]
    load_s = refs[22]
    small = refs[23:39]
    large = refs[39:]
    at = Place(groups, chips)
    n_scan = SmallScan(at, False, small[:8])
    m_scan = SmallScan(at, True, small[8:])
    b_scan = LargeScan(at, False, share, chunks, large[:10])
    c_scan = LargeScan(at, True, share, chunks, large[10:])
    tokens = k_v.shape[1]
    tall = width // 8

    loads = [
        pltpu.make_async_copy(src, dst, load_s.at[i])
        for i, (src, dst) in enumerate(zip(hbm_in, (q_v, k_v, v_v, g_v, st_v, nm_v, gs_v, gn_v)))
    ]
    loads[1].start()
    loads[2].start()
    barrier = pltpu.get_barrier_semaphore()
    partners = [at.core_id()]
    partners += [at.chip_id(at.plane_to(k)) for k in range(len(at.plane))]
    partners += [at.z_id(at.z_to(k)) for k in range(len(at.column))]
    for partner in partners:
        pl.semaphore_signal(barrier, inc=1, device_id=partner, device_id_type=MESH)
    for i in (0, 3, 5, 7, 4, 6):
        loads[i].start()

    upper = lax.broadcasted_iota(jnp.int32, (tokens, tokens), 0) <= lax.broadcasted_iota(
        jnp.int32, (tokens, tokens), 1
    )
    for scan in (b_scan, c_scan):
        scan.own[...] = jnp.zeros(scan.own.shape, F32)
    for scan in (n_scan, m_scan):
        scan.own[...] = jnp.zeros(scan.own.shape, F32)
        scan.total[...] = jnp.zeros(scan.total.shape, F32)
        scan.flat[...] = jnp.zeros(scan.flat.shape, F32)
    den_s[...] = jnp.ones(den_s.shape, F32)
    c_s[...] = jnp.zeros(c_s.shape, F32)

    def tiles(h):
        return slice(h * tall, (h + 1) * tall)

    def rows(h):
        return slice(h * width, (h + 1) * width)

    loads[1].wait()
    b_s[...] = jnp.maximum(k_v[...], 0)
    some = jnp.ones((16, tokens), BF16)
    for h in range(heads):
        n_scan.own[h, :, :width] = mm(some, b_s[rows(h)], NT)[0:1]
    pl.semaphore_wait(barrier, len(partners))
    n_scan.core_send()

    loads[2].wait()
    for h in range(heads):
        state = mm(v_v[rows(h)], b_s[rows(h)], NT)
        b_scan.own[tiles(h), :, :width] = state.reshape(tall, 8, width)
    n_scan.plane_send()
    b_scan.core_send()

    loads[0].wait()
    a_s[...] = jnp.maximum(q_v[...], 0)
    b_scan.plane_send()

    loads[5].wait()
    loads[7].wait()
    for h in range(heads):
        n_scan.total[h, :, :width] = nm_v[h : h + 1]
        m_scan.total[h, :, :width] = gn_v[h : h + 1]
    for h in range(heads):
        scores = jnp.where(upper, mm(b_s[rows(h)], a_s[rows(h)], TN), 0.0)
        den_s[h : h + 1] = 1.0 + jnp.sum(scores, axis=0, keepdims=True)
        pt_s[h] = scores.astype(BF16)
    for h in range(heads):
        num_s[rows(h)] = mm(v_v[rows(h)], pt_s[h], NN)
    n_scan.column_send()

    loads[4].wait()
    loads[6].wait()
    for init, state in ((init_s, st_v), (init_r, gs_v)):
        init[...] = jnp.zeros(init.shape, F32)
        for h in range(heads):
            init[tiles(h), :, :width] = state[h].T.reshape(tall, 8, width)
    b_scan.core_rest()
    init_s[...] = init_s[...] + flag(at.c == 1) * b_scan.other[: heads * tall]
    loads[3].wait()

    n_scan.finish()
    high, low = split(n_scan.flat[:, :width])
    for h in range(heads):
        both = mm(high, a_s[rows(h)], NN) + mm(low, a_s[rows(h)], NN)
        den_s[h : h + 1] = den_s[h : h + 1] + both[h : h + 1]
    den_s[...] = 1.0 / den_s[...]
    for h in range(heads):
        scaled = g_v[rows(h)].astype(F32) * den_s[h : h + 1]
        ub_s[rows(h)], ul_s[rows(h)] = split(scaled)
    for h in range(heads):
        state = mm(ub_s[rows(h)], a_s[rows(h)], NT)
        c_scan.own[tiles(h), :, :width] = state.reshape(tall, 8, width)
    c_scan.core_send()
    for i in range(len(chunks)):
        b_scan.column_send(i)
    for h in range(heads):
        vp_s[rows(h)] = mm(ub_s[rows(h)], pt_s[h], NT)
    c_scan.plane_send()
    for i in range(len(chunks)):
        b_scan.back_send(i)
    c_scan.core_rest()
    init_r[...] = init_r[...] + flag(at.c == 0) * c_scan.other[: heads * tall]
    for i in range(len(chunks)):
        c_scan.column_send(i)
    b_scan.back_pass()
    b_scan.finish()

    for h in range(heads):
        state = (b_scan.result[tiles(h)] + init_s[tiles(h)]).reshape(width, LANES)
        sh_s[rows(h)], sl_s[rows(h)] = split(state)
    for h in range(heads):
        numerator = num_s[rows(h)] + mm(sh_s[rows(h), :width], a_s[rows(h)], NN)
        numerator = numerator + mm(sl_s[rows(h), :width], a_s[rows(h)], NN)
        inverse = den_s[h : h + 1]
        scaled = g_v[rows(h)].astype(F32) * inverse
        c_s[h : h + 1] = -jnp.sum(scaled * (numerator * inverse), axis=0, keepdims=True)
    both = jnp.concatenate(split(c_s[...]), axis=0)
    for h in range(heads):
        part = mm(both, a_s[rows(h)], NT)
        m_scan.own[h, :, :width] = part[h : h + 1] + part[16 + h : 17 + h]
    m_scan.core_send()
    m_scan.plane_send()
    for i in range(len(chunks)):
        c_scan.back_send(i)

    turned = n_scan.flat[...].T
    for h in range(heads):
        here = rows(h)
        c = c_s[h : h + 1]
        mixed = jnp.where(upper, mm(v_v[here], ub_s[here], TN) + c, 0.0).astype(BF16)
        high, low = sh_s[here, :width], sl_s[here, :width]
        part = mm(high, ub_s[here], TN) + mm(low, ub_s[here], TN) + mm(high, ul_s[here], TN)
        part = part + turned[:width, h : h + 1] * c + mm(b_s[here], mixed, NN)
        dq_v[here] = jnp.where(a_s[here] > 0, part, 0.0).astype(BF16)
        kp_s[here] = mm(a_s[here], mixed, NT)
    m_scan.column_send()
    c_scan.back_pass()
    c_scan.finish()

    for h in range(heads):
        state = (c_scan.result[tiles(h)] + init_r[tiles(h)]).reshape(width, LANES)
        sh_s[rows(h)], sl_s[rows(h)] = split(state)
    for h in range(heads):
        here = rows(h)
        high, low = sh_s[here, :width], sl_s[here, :width]
        part = vp_s[here] + mm(high, b_s[here], NN) + mm(low, b_s[here], NN)
        dv_v[here] = part.astype(BF16)
        kp_s[here] = kp_s[here] + mm(high, v_v[here], TN) + mm(low, v_v[here], TN)
    m_scan.finish()
    turned = m_scan.flat[...].T
    for h in range(heads):
        here = rows(h)
        part = jnp.where(b_s[here] > 0, kp_s[here] + turned[:width, h : h + 1], 0.0)
        dk_v[here] = part.astype(BF16)
    for scan in (n_scan, b_scan, m_scan, c_scan):
        scan.drain()


def small_scratch(groups, chips, heads):
    one = (heads, 1, LANES)
    return [
        pltpu.VMEM(one, F32),
        pltpu.VMEM(one, F32),
        pltpu.VMEM(one, F32),
        pltpu.VMEM((chips, *one), F32),
        pltpu.VMEM((groups, *one), F32),
        pltpu.VMEM(one, F32),
        pltpu.VMEM((16, LANES), F32),
        pltpu.SemaphoreType.DMA((6,)),
    ]


def large_scratch(groups, chips, share, chunks):
    whole = pltpu.VMEM((2 * chips * share, 8, LANES), F32)
    plane = pltpu.VMEM((chips, share, 8, LANES), F32)
    sem = pltpu.SemaphoreType.DMA
    return [
        whole,
        whole,
        plane,
        plane,
        pltpu.VMEM((groups, share, 8, LANES), F32),
        plane,
        whole,
        sem((2, 3)),
        sem((len(chunks), 5)),
        sem((math.isqrt(chips),)),
    ]


def place(*refs):
    sems = refs[6]
    copies = [pltpu.make_async_copy(refs[i], refs[3 + i], sems.at[i]) for i in range(3)]
    for copy in copies:
        copy.start()
    for copy in copies:
        copy.wait()


def per_device(groups, chips, *args):
    args = [x.T for x in args[:4]] + list(args[4:])
    columns, tokens = args[0].shape
    heads, width = args[4].shape[:2]
    share = -(-(heads * width // 8) // (2 * chips))
    chunks = ((0, share),)
    token = pltpu.VMEM((columns, tokens), BF16)
    wide = pltpu.VMEM((columns, tokens), F32)
    state = pltpu.VMEM((heads, width, width), F32)
    norm = pltpu.VMEM((heads, width), F32)
    one = pltpu.VMEM((16, tokens), F32)
    init = pltpu.VMEM((heads * width // 8, 8, LANES), F32)
    sem = pltpu.SemaphoreType.DMA
    scratch = [token] * 4 + [state, norm, state, norm]
    scratch += [token] * 4 + [pltpu.VMEM((columns, LANES), BF16)] * 2
    scratch += [pltpu.VMEM((heads, tokens, tokens), BF16)]
    scratch += [wide] * 3 + [one] * 2 + [init] * 2 + [sem((8,))]
    scratch += small_scratch(groups, chips, heads) * 2 + large_scratch(groups, chips, share, chunks) * 2
    outs = pl.pallas_call(
        functools.partial(kernel, groups, chips, heads, width, share, chunks),
        out_shape=[pltpu.VMEM((columns, tokens), BF16)] * 3,
        in_specs=[pl.BlockSpec(memory_space=pl.ANY)] * 8,
        out_specs=[pl.BlockSpec(memory_space=pltpu.VMEM)] * 3,
        scratch_shapes=scratch,
        compiler_params=pltpu.CompilerParams(
            collective_id=0, has_side_effects=True, vmem_limit_bytes=60 * 2**20
        ),
        name="scan_kernel",
    )(*args)
    outs = pl.pallas_call(
        place,
        out_shape=[jax.ShapeDtypeStruct((columns, tokens), BF16)] * 3,
        in_specs=[pl.BlockSpec(memory_space=pl.ANY)] * 3,
        out_specs=[pl.BlockSpec(memory_space=pl.ANY)] * 3,
        scratch_shapes=[sem((3,))],
        compiler_params=pltpu.CompilerParams(vmem_limit_bytes=2**20),
        name="place_outputs",
    )(*outs)
    return tuple(x.T for x in outs)


def solution(mesh):
    groups, chips = mesh.shape["grp"], mesh.shape["seq"] // 2
    tokens = P(("grp", "seq"), None)
    return jax.shard_map(
        functools.partial(per_device, groups, chips),
        mesh=mesh,
        in_specs=(tokens,) * 4 + (P(),) * 4,
        out_specs=(tokens,) * 3,
        check_vma=False,
    )
```

```python
import functools
import math

import jax
import jax.numpy as jnp
from jax import lax
from jax.experimental import pallas as pl
from jax.experimental.pallas import tpu as pltpu
from jax.sharding import PartitionSpec as P

MESH = pl.DeviceIdType.MESH
F32 = jnp.float32
BF16 = jnp.bfloat16
NN = (((1,), (0,)), ((), ()))
NT = (((1,), (1,)), ((), ()))
TN = (((0,), (0,)), ((), ()))
LANES = 128


def mm(x, y, dims):
    return lax.dot_general(x, y, dims, preferred_element_type=F32)


def split(x):
    high = x.astype(BF16)
    return high, (x - high.astype(F32)).astype(BF16)


class Place:
    def __init__(self, groups, chips):
        self.groups, self.chips = groups, chips
        self.side = math.isqrt(chips)
        self.z = lax.axis_index("grp")
        seq = lax.axis_index("seq")
        self.p, self.c = seq // 2, seq % 2
        self.y, self.x = self.p // self.side, self.p % self.side
        side = self.side
        offsets = [(dy, dx) for dy in range(side) for dx in range(side) if dy or dx]
        self.plane = sorted(offsets, key=lambda o: min(o[0], side - o[0]) + min(o[1], side - o[1]))
        self.far_rows = sorted(range(side), key=lambda d: -min(d, side - d))
        self.column = sorted(range(1, groups), key=lambda d: min(d, groups - d))

    def chip(self, offset, sign):
        side = self.side
        y = (self.y + sign * offset[0] + side) % side
        x = (self.x + sign * offset[1] + side) % side
        return y * side + x

    def plane_to(self, k):
        return self.chip(self.plane[k], 1)

    def plane_from(self, k):
        return self.chip(self.plane[k], -1)

    def z_to(self, k):
        return (self.z + self.column[k]) % self.groups

    def z_from(self, k):
        return (self.z + self.groups - self.column[k]) % self.groups

    def chip_id(self, p):
        return (self.z, p * 2 + self.c)

    def z_id(self, z):
        return (z, self.p * 2 + self.c)

    def core_id(self):
        return (self.z, self.p * 2 + 1 - self.c)


def remote(src, dst, send, recv, device):
    return pltpu.make_async_remote_copy(
        src_ref=src, dst_ref=dst, send_sem=send, recv_sem=recv, device_id=device, device_id_type=MESH
    )


def flag(condition):
    return condition.astype(jnp.int32).astype(F32)


def arrived(ref, sem):
    pltpu.make_async_copy(ref, ref, sem).wait()


def z_send(at, later, start):
    for k in reversed(range(len(at.column))):
        offset = at.column[k]
        target = at.z - offset if later else at.z + offset
        inside = target >= 0 if later else target < at.groups

        @pl.when(inside)
        def _():
            start(target)


def z_arrived(at, below, view, sem):
    for n in range(1, at.groups):

        @pl.when(at.z == (n if below else at.groups - 1 - n))
        def _():
            arrived(view(n), sem)


class SmallScan:
    def __init__(self, at, later, refs):
        self.at, self.later = at, later
        self.own, self.other, self.chip, self.plane, self.column, self.total, self.flat = refs[:7]
        self.sems = refs[7]
        self.reached = (lambda i, me: i > me) if later else (lambda i, me: i < me)

    def core_send(self):
        sems = self.sems
        remote(self.own, self.other, sems.at[0], sems.at[1], self.at.core_id()).start()

    def plane_send(self):
        at, sems = self.at, self.sems
        arrived(self.other, sems.at[1])
        both = self.own[...] + self.other[...]
        self.chip[...] = both
        for k in reversed(range(len(at.plane))):
            device = at.chip_id(at.plane_to(k))
            remote(self.chip, self.plane.at[at.p], sems.at[2], sems.at[3], device).start()
        self.plane[at.p] = both

    def column_send(self):
        at, sems = self.at, self.sems
        arrived(self.plane.at[: at.chips - 1], sems.at[3])
        everything = self.plane[0]
        for p in range(1, at.chips):
            everything = everything + self.plane[p]
        self.column[at.z] = everything
        mine = self.column.at[at.z]
        z_send(
            at,
            self.later,
            lambda z: remote(mine, mine, sems.at[4], sems.at[5], at.z_id(z)).start(),
        )
        near = flag(at.c == (0 if self.later else 1)) * self.other[...]
        for p in range(at.chips):
            near = near + flag(self.reached(p, at.p)) * self.plane[p]
        self.total[...] = self.total[...] + near

    def finish(self):
        at = self.at
        z_arrived(at, not self.later, lambda n: self.column.at[:n], self.sems.at[5])
        far = jnp.where(self.reached(0, at.z), self.column[0], 0.0)
        for z in range(1, at.groups):
            far = far + jnp.where(self.reached(z, at.z), self.column[z], 0.0)
        self.total[...] = self.total[...] + far
        for h in range(self.total.shape[0]):
            self.flat[h : h + 1, :] = self.total[h]

    def drain(self):
        at, sems = self.at, self.sems
        arrived(self.own, sems.at[0])
        arrived(self.plane.at[: at.chips - 1], sems.at[2])
        z_arrived(at, self.later, lambda n: self.column.at[:n], sems.at[4])


class LargeScan:
    def __init__(self, at, later, share, chunks, refs):
        self.at, self.later, self.share, self.chunks = at, later, share, chunks
        self.own, self.other, self.chip, self.plane, self.column, self.back, self.result = refs[:7]
        self.core_s, self.chunk_s, self.back_s = refs[7:]
        self.half = share * at.chips
        self.reached = (lambda i, me: i > me) if later else (lambda i, me: i < me)

    def piece(self, core, p, chunk=None):
        first, count = (0, self.share) if chunk is None else self.chunks[chunk]
        return pl.ds((core * self.at.chips + p) * self.share + first, count)

    def part(self, chunk):
        first, count = self.chunks[chunk]
        return pl.ds(first, count)

    def core_copy(self, k, core):
        half = pl.ds(core * self.half, self.half)
        sems = self.core_s
        return remote(
            self.own.at[half], self.other.at[half], sems.at[0, k], sems.at[1, k], self.at.core_id()
        )

    def core_send(self):
        self.core_copy(0, 1 - self.at.c).start()

    def core_rest(self):
        self.core_copy(1, 1 - self.at.c).wait_recv()

    def plane_send(self):
        at = self.at
        self.core_copy(0, at.c).wait_recv()
        for i in range(len(self.chunks)):
            part, sems = self.part(i), self.chunk_s.at[i]
            for k in reversed(range(len(at.plane))):
                target = at.plane_to(k)
                piece = self.piece(at.c, target, i)
                self.chip[target, part] = self.own[piece] + self.other[piece]
                remote(
                    self.chip.at[target, part],
                    self.plane.at[at.p, part],
                    sems.at[0],
                    sems.at[1],
                    at.chip_id(target),
                ).start()
        self.core_copy(1, at.c).start()
        piece = self.piece(at.c, at.p)
        self.plane[at.p] = self.own[piece] + self.other[piece]

    def column_send(self, i):
        at = self.at
        part, sems = self.part(i), self.chunk_s.at[i]
        arrived(self.plane.at[: at.chips - 1, part], sems.at[1])
        total = self.plane[0, part]
        for p in range(1, at.chips):
            total = total + self.plane[p, part]
        self.column[at.z, part] = total
        mine = self.column.at[at.z, part]
        z_send(
            at,
            self.later,
            lambda z: remote(mine, mine, sems.at[2], sems.at[3], at.z_id(z)).start(),
        )
        order = list(range(at.chips))
        if self.later:
            order.reverse()
        running = jnp.zeros((self.chunks[i][1], *self.column.shape[2:]), F32)
        for p in order:
            self.back[p, part] = running
            running = running + self.plane[p, part]

    def back_send(self, i):
        at = self.at
        part, sems = self.part(i), self.chunk_s.at[i]
        z_arrived(at, not self.later, lambda n: self.column.at[:n, part], sems.at[3])
        far = jnp.where(self.reached(0, at.z), self.column[0, part], 0.0)
        for z in range(1, at.groups):
            far = far + jnp.where(self.reached(z, at.z), self.column[z, part], 0.0)
        for k in reversed(range(len(at.plane))):
            target = at.plane_to(k)
            self.back[target, part] = self.back[target, part] + far
            remote(
                self.back.at[target, part],
                self.result.at[self.piece(at.c, at.p, i)],
                sems.at[4],
                self.back_s.at[at.plane[k][0]],
                at.chip_id(target),
            ).start()
        self.result[self.piece(at.c, at.p, i)] = self.back[at.p, part] + far

    def back_pass(self):
        at = self.at
        for dy in reversed(at.far_rows):
            first = at.c * at.chips + (at.y + at.side - dy) % at.side * at.side
            row = self.result.at[pl.ds(first * self.share, at.side * self.share)]
            count = at.side if dy else at.side - 1
            arrived(self.result.at[pl.ds(first * self.share, count * self.share)], self.back_s.at[dy])
            remote(row, row, self.core_s.at[0, 2], self.core_s.at[1, 2], at.core_id()).start()

    def finish(self):
        half = pl.ds((1 - self.at.c) * self.half, self.half)
        arrived(self.result.at[half], self.core_s.at[1, 2])

    def drain(self):
        at = self.at
        half = pl.ds(0, self.half)
        for k in range(2):
            arrived(self.own.at[half], self.core_s.at[0, k])
        arrived(self.result.at[half], self.core_s.at[0, 2])
        for i in range(len(self.chunks)):
            part, sems = self.part(i), self.chunk_s.at[i]
            arrived(self.plane.at[: at.chips - 1, part], sems.at[0])
            z_arrived(at, self.later, lambda n: self.column.at[:n, part], sems.at[2])
            arrived(self.plane.at[: at.chips - 1, part], sems.at[4])


def kernel(groups, chips, heads, width, share, chunks, *refs):
    hbm_in, (dq_v, dk_v, dv_v), refs = refs[:8], refs[8:11], refs[11:]
    q_v, k_v, v_v, g_v, st_v, nm_v, gs_v, gn_v = refs[:8]
    a_s, b_s, ub_s, ul_s, sh_s, sl_s, pt_s = refs[8:15]
    num_s, kp_s, vp_s, den_s, c_s, init_s, init_r = refs[15:22]
    load_s = refs[22]
    small = refs[23:39]
    large = refs[39:]
    at = Place(groups, chips)
    n_scan = SmallScan(at, False, small[:8])
    m_scan = SmallScan(at, True, small[8:])
    b_scan = LargeScan(at, False, share, chunks, large[:10])
    c_scan = LargeScan(at, True, share, chunks, large[10:])
    tokens = k_v.shape[1]
    tall = width // 8

    loads = [
        pltpu.make_async_copy(src, dst, load_s.at[i])
        for i, (src, dst) in enumerate(zip(hbm_in, (q_v, k_v, v_v, g_v, st_v, nm_v, gs_v, gn_v)))
    ]
    loads[1].start()
    loads[2].start()
    barrier = pltpu.get_barrier_semaphore()
    partners = [at.core_id()]
    partners += [at.chip_id(at.plane_to(k)) for k in range(len(at.plane))]
    partners += [at.z_id(at.z_to(k)) for k in range(len(at.column))]
    for partner in partners:
        pl.semaphore_signal(barrier, inc=1, device_id=partner, device_id_type=MESH)
    for i in (0, 3, 5, 7, 4, 6):
        loads[i].start()

    upper = lax.broadcasted_iota(jnp.int32, (tokens, tokens), 0) <= lax.broadcasted_iota(
        jnp.int32, (tokens, tokens), 1
    )
    for scan in (b_scan, c_scan):
        scan.own[...] = jnp.zeros(scan.own.shape, F32)
    for scan in (n_scan, m_scan):
        scan.own[...] = jnp.zeros(scan.own.shape, F32)
        scan.total[...] = jnp.zeros(scan.total.shape, F32)
        scan.flat[...] = jnp.zeros(scan.flat.shape, F32)
    den_s[...] = jnp.ones(den_s.shape, F32)
    c_s[...] = jnp.zeros(c_s.shape, F32)

    def tiles(h):
        return slice(h * tall, (h + 1) * tall)

    def rows(h):
        return slice(h * width, (h + 1) * width)

    loads[1].wait()
    b_s[...] = jnp.maximum(k_v[...], 0)
    some = jnp.ones((16, tokens), BF16)
    for h in range(heads):
        n_scan.own[h, :, :width] = mm(some, b_s[rows(h)], NT)[0:1]
    pl.semaphore_wait(barrier, len(partners))
    n_scan.core_send()

    loads[2].wait()
    for h in range(heads):
        state = mm(v_v[rows(h)], b_s[rows(h)], NT)
        b_scan.own[tiles(h), :, :width] = state.reshape(tall, 8, width)
    n_scan.plane_send()
    b_scan.core_send()

    loads[0].wait()
    a_s[...] = jnp.maximum(q_v[...], 0)
    b_scan.plane_send()

    loads[5].wait()
    loads[7].wait()
    for h in range(heads):
        n_scan.total[h, :, :width] = nm_v[h : h + 1]
        m_scan.total[h, :, :width] = gn_v[h : h + 1]
    for h in range(heads):
        scores = jnp.where(upper, mm(b_s[rows(h)], a_s[rows(h)], TN), 0.0)
        den_s[h : h + 1] = 1.0 + jnp.sum(scores, axis=0, keepdims=True)
        pt_s[h] = scores.astype(BF16)
    for h in range(heads):
        num_s[rows(h)] = mm(v_v[rows(h)], pt_s[h], NN)
    n_scan.column_send()

    loads[4].wait()
    loads[6].wait()
    for init, state in ((init_s, st_v), (init_r, gs_v)):
        init[...] = jnp.zeros(init.shape, F32)
        for h in range(heads):
            init[tiles(h), :, :width] = state[h].T.reshape(tall, 8, width)
    b_scan.core_rest()
    init_s[...] = init_s[...] + flag(at.c == 1) * b_scan.other[: heads * tall]
    loads[3].wait()

    n_scan.finish()
    high, low = split(n_scan.flat[:, :width])
    for h in range(heads):
        both = mm(high, a_s[rows(h)], NN) + mm(low, a_s[rows(h)], NN)
        den_s[h : h + 1] = den_s[h : h + 1] + both[h : h + 1]
    den_s[...] = 1.0 / den_s[...]
    for h in range(heads):
        scaled = g_v[rows(h)].astype(F32) * den_s[h : h + 1]
        ub_s[rows(h)], ul_s[rows(h)] = split(scaled)
    for h in range(heads):
        state = mm(ub_s[rows(h)], a_s[rows(h)], NT)
        c_scan.own[tiles(h), :, :width] = state.reshape(tall, 8, width)
    c_scan.core_send()
    for i in range(len(chunks)):
        b_scan.column_send(i)
    for h in range(heads):
        vp_s[rows(h)] = mm(ub_s[rows(h)], pt_s[h], NT)
    c_scan.plane_send()
    for i in range(len(chunks)):
        b_scan.back_send(i)
    c_scan.core_rest()
    init_r[...] = init_r[...] + flag(at.c == 0) * c_scan.other[: heads * tall]
    for i in range(len(chunks)):
        c_scan.column_send(i)
    b_scan.back_pass()
    b_scan.finish()

    for h in range(heads):
        state = (b_scan.result[tiles(h)] + init_s[tiles(h)]).reshape(width, LANES)
        sh_s[rows(h)], sl_s[rows(h)] = split(state)
    for h in range(heads):
        numerator = num_s[rows(h)] + mm(sh_s[rows(h), :width], a_s[rows(h)], NN)
        numerator = numerator + mm(sl_s[rows(h), :width], a_s[rows(h)], NN)
        inverse = den_s[h : h + 1]
        scaled = g_v[rows(h)].astype(F32) * inverse
        c_s[h : h + 1] = -jnp.sum(scaled * (numerator * inverse), axis=0, keepdims=True)
    both = jnp.concatenate(split(c_s[...]), axis=0)
    for h in range(heads):
        part = mm(both, a_s[rows(h)], NT)
        m_scan.own[h, :, :width] = part[h : h + 1] + part[16 + h : 17 + h]
    m_scan.core_send()
    m_scan.plane_send()
    for i in range(len(chunks)):
        c_scan.back_send(i)

    turned = n_scan.flat[...].T
    for h in range(heads):
        here = rows(h)
        c = c_s[h : h + 1]
        mixed = jnp.where(upper, mm(v_v[here], ub_s[here], TN) + c, 0.0).astype(BF16)
        high, low = sh_s[here, :width], sl_s[here, :width]
        part = mm(high, ub_s[here], TN) + mm(low, ub_s[here], TN) + mm(high, ul_s[here], TN)
        part = part + turned[:width, h : h + 1] * c + mm(b_s[here], mixed, NN)
        dq_v[here] = jnp.where(a_s[here] > 0, part, 0.0).astype(BF16)
        kp_s[here] = mm(a_s[here], mixed, NT)
    m_scan.column_send()
    c_scan.back_pass()
    c_scan.finish()

    for h in range(heads):
        state = (c_scan.result[tiles(h)] + init_r[tiles(h)]).reshape(width, LANES)
        sh_s[rows(h)], sl_s[rows(h)] = split(state)
    for h in range(heads):
        here = rows(h)
        high, low = sh_s[here, :width], sl_s[here, :width]
        part = vp_s[here] + mm(high, b_s[here], NN) + mm(low, b_s[here], NN)
        dv_v[here] = part.astype(BF16)
        kp_s[here] = kp_s[here] + mm(high, v_v[here], TN) + mm(low, v_v[here], TN)
    m_scan.finish()
    turned = m_scan.flat[...].T
    for h in range(heads):
        here = rows(h)
        part = jnp.where(b_s[here] > 0, kp_s[here] + turned[:width, h : h + 1], 0.0)
        dk_v[here] = part.astype(BF16)
    for scan in (n_scan, b_scan, m_scan, c_scan):
        scan.drain()


def small_scratch(groups, chips, heads):
    one = (heads, 1, LANES)
    return [
        pltpu.VMEM(one, F32),
        pltpu.VMEM(one, F32),
        pltpu.VMEM(one, F32),
        pltpu.VMEM((chips, *one), F32),
        pltpu.VMEM((groups, *one), F32),
        pltpu.VMEM(one, F32),
        pltpu.VMEM((16, LANES), F32),
        pltpu.SemaphoreType.DMA((6,)),
    ]


def large_scratch(groups, chips, share, chunks):
    whole = pltpu.VMEM((2 * chips * share, 8, LANES), F32)
    plane = pltpu.VMEM((chips, share, 8, LANES), F32)
    sem = pltpu.SemaphoreType.DMA
    return [
        whole,
        whole,
        plane,
        plane,
        pltpu.VMEM((groups, share, 8, LANES), F32),
        plane,
        whole,
        sem((2, 3)),
        sem((len(chunks), 5)),
        sem((math.isqrt(chips),)),
    ]


def place(*refs):
    sems = refs[6]
    copies = [pltpu.make_async_copy(refs[i], refs[3 + i], sems.at[i]) for i in range(3)]
    for copy in copies:
        copy.start()
    for copy in copies:
        copy.wait()


def per_device(groups, chips, *args):
    args = [x.T for x in args[:4]] + list(args[4:])
    columns, tokens = args[0].shape
    heads, width = args[4].shape[:2]
    share = -(-(heads * width // 8) // (2 * chips))
    chunks = ((0, share),)
    token = pltpu.VMEM((columns, tokens), BF16)
    wide = pltpu.VMEM((columns, tokens), F32)
    state = pltpu.VMEM((heads, width, width), F32)
    norm = pltpu.VMEM((heads, width), F32)
    one = pltpu.VMEM((16, tokens), F32)
    init = pltpu.VMEM((heads * width // 8, 8, LANES), F32)
    sem = pltpu.SemaphoreType.DMA
    scratch = [token] * 4 + [state, norm, state, norm]
    scratch += [token] * 4 + [pltpu.VMEM((columns, LANES), BF16)] * 2
    scratch += [pltpu.VMEM((heads, tokens, tokens), BF16)]
    scratch += [wide] * 3 + [one] * 2 + [init] * 2 + [sem((8,))]
    scratch += small_scratch(groups, chips, heads) * 2 + large_scratch(groups, chips, share, chunks) * 2
    outs = pl.pallas_call(
        functools.partial(kernel, groups, chips, heads, width, share, chunks),
        out_shape=[pltpu.VMEM((columns, tokens), BF16)] * 3,
        in_specs=[pl.BlockSpec(memory_space=pl.ANY)] * 8,
        out_specs=[pl.BlockSpec(memory_space=pltpu.VMEM)] * 3,
        scratch_shapes=scratch,
        compiler_params=pltpu.CompilerParams(
            collective_id=0, has_side_effects=True, vmem_limit_bytes=60 * 2**20
        ),
        name="scan_kernel",
    )(*args)
    outs = pl.pallas_call(
        place,
        out_shape=[jax.ShapeDtypeStruct((columns, tokens), BF16)] * 3,
        in_specs=[pl.BlockSpec(memory_space=pl.ANY)] * 3,
        out_specs=[pl.BlockSpec(memory_space=pl.ANY)] * 3,
        scratch_shapes=[sem((3,))],
        compiler_params=pltpu.CompilerParams(vmem_limit_bytes=2**20),
        name="place_outputs",
    )(*outs)
    return tuple(x.T for x in outs)


def solution(mesh):
    groups, chips = mesh.shape["grp"], mesh.shape["seq"] // 2
    tokens = P(("grp", "seq"), None)
    return jax.shard_map(
        functools.partial(per_device, groups, chips),
        mesh=mesh,
        in_specs=(tokens,) * 4 + (P(),) * 4,
        out_specs=(tokens,) * 3,
        check_vma=False,
    )
```
